512 devices in a mesh: lon: 16 (over y, x), lat: 32 (over z, core).
Axes of the slice: x: 4, y: 4, z: 16, core: 2. Of those that a mesh axis runs over, the one named last changes fastest.
Arguments:
- vorticity: float32 [8, 2, 768, 3072], P(None, None, 'lat', 'lon'), may hold values from -6 to 6
- legendre_table: float32 [768, 512, 1025], P('lat', 'lon'), may hold values from -0.15625 to 0.15625
- pair_slots: int32 [512], replicated, may hold values from 0 to 511, each once
- diffusion: float32 [8], replicated, may hold values from 0.3 to 3
Outputs:
- spectrum: float32 [512, 8, 2, 1025], P('lon')
The draws below stay inside these ranges and needn't reach their ends.
Inputs may be any that keep to these rules, and one draw needn't show every extreme that they name: Each pair appears in exactly one slot; slot s holds the wavenumbers pair_slots[s] and 1023 - pair_slots[s].
All inputs are finite; a program needn't handle non-finite values.
Results may differ from the reference program's by a relative error of at most 0.0003.
Values sent between devices are 32-bit elements; how exact they have to be, the bound alone decides.
A program may use at most 64 MiB of HBM per device.

```python
import math
import jax
import jax.numpy as jnp
from jax import lax

WAVES = 1024
NHALF = 768
NLON = 3072
LEVELS = 8
PAIRS = 512
COLS = 1025


def steps_of(key, dims, split, smallest, largest):
    factor_of = 1.0
    for axis_at, parts in split:
        steps = jax.random.uniform(jax.random.fold_in(jax.random.fold_in(key, 6), axis_at), (parts,), jnp.float32, smallest / len(split), largest / len(split))
        factor_of = factor_of * jnp.repeat(jnp.exp(steps), dims[axis_at] // parts).reshape((-1,) + (1,) * (len(dims) - 1 - axis_at))
    return factor_of


def centred(rng, shape, spread, limit, pieces=(), kind=jnp.bfloat16):
    array = spread * jax.random.normal(rng, shape, jnp.float32)
    if pieces:
        array = array * steps_of(rng, shape, pieces, -0.22, 0.18)
    return jnp.clip(array, -limit, limit).astype(kind)


def setup_inputs(seed: int = 0) -> dict:
    key_list = jax.random.split(jax.random.key(seed), 5)
    return {
        "vorticity": centred(key_list[0], (LEVELS, 2, NHALF, NLON), 1.0, 6.0, ((2, 32), (3, 16)), jnp.float32),
        "legendre_table": centred(key_list[1], (NHALF, PAIRS, COLS), (2 * NHALF) ** -0.5, 0.15625, ((0, 32), (1, 16)), jnp.float32),
        "pair_slots": jax.random.permutation(key_list[2], PAIRS).astype(jnp.int32),
        "diffusion": jnp.clip(jnp.exp(jax.random.uniform(key_list[3], (LEVELS,), jnp.float32, math.log(0.3), math.log(3.0))), 0.3, 3.0),
    }


def reference(vorticity, legendre_table, pair_slots, diffusion):
    spectral = jnp.fft.rfft(vorticity, axis=-1)[..., :WAVES]
    norm_scale = 1.0 / math.sqrt(NLON)
    four_re = jnp.real(spectral) * norm_scale
    four_im = jnp.imag(spectral) * norm_scale
    fourier = jnp.stack([four_re, four_im], axis=-1)
    columns = jnp.arange(WAVES + 1, dtype=jnp.int32)
    degree_scale = float((WAVES - 1) * WAVES)

    def one_slot(inputs):
        slot_id, pair_id = inputs
        first_len = WAVES - pair_id
        second = columns >= first_len
        offset = jnp.where(second, columns - first_len, columns)
        odd_mask = offset % 2 == 1
        wave_table = jnp.take(legendre_table, slot_id, axis=1)

        def project_wave(wave_data):
            symmetric = wave_data[:, 0] + wave_data[:, 1]
            antisymmetric = wave_data[:, 0] - wave_data[:, 1]
            sym_out = jnp.einsum('ljr,jc->lrc', symmetric, wave_table, precision=lax.Precision.HIGHEST)
            anti_out = jnp.einsum('ljr,jc->lrc', antisymmetric, wave_table, precision=lax.Precision.HIGHEST)
            return jnp.where(odd_mask, anti_out, sym_out)
        first_wave = jnp.take(fourier, pair_id, axis=3)
        second_wave = jnp.take(fourier, WAVES - 1 - pair_id, axis=3)
        result = jnp.where(second, project_wave(second_wave), project_wave(first_wave))
        degree = jnp.where(second, columns - 1, pair_id + columns).astype(jnp.float32)
        degree_ratio = degree * (degree + 1.0) / degree_scale
        damping = 1.0 / (1.0 + diffusion[:, None, None] * (degree_ratio ** 2)[None, None, :])
        return result * damping
    return lax.map(one_slot, (jnp.arange(PAIRS, dtype=jnp.int32), pair_slots))
```

```python
import functools
import math

import jax
import jax.numpy as jnp
import numpy as np
from jax import lax
from jax.experimental import pallas as pl
from jax.experimental.pallas import tpu as pltpu
from jax.sharding import PartitionSpec as P

MESH = pl.DeviceIdType.MESH
F32 = jnp.float32
BF16 = jnp.bfloat16


def real_dft(parts):
    n = len(parts)
    if n == 1:
        return [(parts[0], None)]
    even, odd = real_dft(parts[0::2]), real_dft(parts[1::2])
    out = [None] * (n // 2 + 1)
    for k in range(n // 4 + 1):
        er, ei = even[k]
        orr, oi = odd[k]
        if k == 0:
            out[0] = (er + orr, None)
            out[n // 2] = (er - orr, None)
        elif 4 * k == n:
            out[k] = (er, -orr)
        else:
            c, s = math.cos(2 * math.pi * k / n), math.sin(2 * math.pi * k / n)
            tr, ti = c * orr, -s * orr
            if oi is not None:
                tr, ti = tr + s * oi, ti + c * oi
            ei = 0.0 if ei is None else ei
            out[k] = (er + tr, ei + ti)
            out[n // 2 - k] = (er - tr, ti - ei)
    return out


def class_blocks(k, blocks):
    rows = [(0, k, 0, 0), (0, k, 1, 0), (1, blocks - 1 - k, 0, 0), (1, blocks - 1 - k, 1, 0)]
    if 0 < k < blocks // 2:
        rows += [(0, blocks - k, 0, 1), (0, blocks - k, 1, 1), (1, k - 1, 0, 1), (1, k - 1, 1, 1)]
    return rows


def twiddles(blocks, width, waves):
    full = blocks * width
    per_class = waves // 2 // blocks
    half = blocks // 2
    table = np.zeros((2 * half, 8 * per_class, width))
    position = np.arange(width)
    for k in range(half + 1):
        for at, (second, residue, part, conj) in enumerate(class_blocks(k, blocks)):
            pair = np.arange(per_class) * blocks + residue
            wave = waves - 1 - pair if second else pair
            angle = 2 * np.pi * ((wave[:, None] * position[None, :]) % full) / full
            cos, sin = np.cos(angle) / math.sqrt(full), np.sin(angle) / math.sqrt(full)
            sign = -1.0 if conj else 1.0
            rows = slice(at * per_class, (at + 1) * per_class)
            table[k, rows] = -sin if part else cos
            if 0 < k < half:
                table[half + k, rows] = sign * (cos if part else sin)
    return table.astype(np.float32)


def split(values):
    high = values.astype(BF16)
    return high, (values - high.astype(F32)).astype(BF16)


def dot_t(a, b):
    return lax.dot_general(a, b, (((1,), (1,)), ((), ())), preferred_element_type=F32)


def kernel(
    dims, pair_ref, diff_ref, vort_hbm, table_hbm, twid_hbm, out_hbm,
    vort, table, tail, twid, twid_split, cat, s1, r1, g, s2, r2, part, sib, ring, final,
    load_sem, tab_sem, out_sem, s1_send, s1_recv, s2_send, s2_recv, sib_send, sib_recv,
    rs_send, rs_recv, ag_send, ag_recv, as_send, as_recv,
):
    blocks, depth, levels, band, width, slots, waves, cw = dims
    half, hops = blocks // 2, depth // 2
    tiles = waves // cw
    pad = 32
    per_class = waves // 2 // blocks
    main_rows = 2 * tiles * levels
    pieces = ((0, main_rows // 2, hops), (main_rows // 2, main_rows // 2 + levels, hops - 1))

    me = lax.axis_index("lon")
    lat = lax.axis_index("lat")
    z, core = lat // 2, lat % 2
    other = 1 - core

    def at_z(step):
        return lax.rem(z + step + depth, depth)

    def z_device(step):
        return (me, at_z(step) * 2 + core)

    sibling = (me, z * 2 + other)

    load = pltpu.make_async_copy(vort_hbm, vort, load_sem.at[0])
    load.start()
    load_twid = pltpu.make_async_copy(twid_hbm, twid, load_sem.at[1])
    load_twid.start()

    def table_copy(k):
        if k == tiles:
            return pltpu.make_async_copy(table_hbm.at[:, pl.ds(waves, 1)], tail, tab_sem.at[k])
        return pltpu.make_async_copy(
            table_hbm.at[:, pl.ds(k * cw, cw)], table.at[k, pl.ds(0, band * slots)], tab_sem.at[k]
        )

    for k in range(tiles + 1):
        table_copy(k).start()

    barrier = pltpu.get_barrier_semaphore()

    def greet(k, carry):
        peer = lax.rem(me + k, blocks)
        pl.semaphore_signal(barrier, inc=1, device_id=(peer, lat), device_id_type=MESH)
        return carry

    lax.fori_loop(1, blocks, greet, 0)
    for target in (z_device(1), z_device(-1), sibling):
        pl.semaphore_signal(barrier, inc=1, device_id=target, device_id_type=MESH)

    load.wait()
    for level in range(levels):
        north = vort[pl.ds(2 * level * band, band), :]
        south = vort[pl.ds((2 * level + 1) * band, band), :]
        s1[level] = north + south
        s1[levels + level] = north - south

    pl.semaphore_wait(barrier, blocks + 2)

    def send1(k):
        peer = lax.rem(me + k, blocks)
        return pltpu.make_async_remote_copy(
            src_ref=s1.at[peer], dst_ref=r1.at[me], send_sem=s1_send.at[peer],
            recv_sem=s1_recv.at[me], device_id=(peer, lat), device_id_type=MESH,
        )

    def recv1(k):
        peer = lax.rem(me + k, blocks)
        return pltpu.make_async_remote_copy(
            src_ref=s1.at[peer], dst_ref=r1.at[peer], send_sem=s1_send.at[peer],
            recv_sem=s1_recv.at[peer], device_id=(peer, lat), device_id_type=MESH,
        )

    def loop(low, high, body):
        def step(k, carry):
            body(k)
            return carry

        lax.fori_loop(low, high, step, 0)

    loop(1, blocks, lambda k: send1(k).start())
    r1[me] = s1[me]

    for k in range(tiles + 1):
        table_copy(k).wait()
    table[tiles, pl.ds(0, band * slots), :] = jnp.broadcast_to(tail[...], (band * slots, cw))

    def stack_table(s):
        for k in range(tiles + 1):
            rows = table[k, pl.ds(s, band, stride=slots), :]
            if band < pad:
                rows = jnp.concatenate([rows, jnp.zeros((pad - band, cw), F32)], axis=0)
            high, low = split(rows)
            lanes = pl.ds(k * cw, cw)
            cat[s, pl.ds(0, pad), lanes] = high
            cat[s, pl.ds(pad, pad), lanes] = high
            cat[s, pl.ds(2 * pad, pad), lanes] = low

    loop(0, slots, stack_table)

    load_twid.wait()

    def split_twiddles(k):
        high, low = split(twid[k])
        twid_split[0, k] = high
        twid_split[1, k] = low

    loop(0, 2 * half, split_twiddles)
    loop(1, blocks, lambda k: recv1(k).wait_recv())

    spectrum = real_dft([r1[a] for a in range(blocks)])
    for k in range(half + 1):
        rows = class_blocks(k, blocks)
        count = len(rows) * per_class
        total = None
        for number, value in ((k, spectrum[k][0]), (half + k, spectrum[k][1])):
            if value is None:
                continue
            if band < pad:
                value = jnp.concatenate([value, jnp.zeros((pad - band, width), F32)], axis=0)
            high, low = split(value)
            w_high = twid_split[0, number, pl.ds(0, count), :]
            w_low = twid_split[1, number, pl.ds(0, count), :]
            term = dot_t(w_high, high) + (dot_t(w_high, low) + dot_t(w_low, high))
            total = term if total is None else total + term
        for at, (second, residue, which, _) in enumerate(rows):
            g[pl.ds(residue * per_class, per_class), pl.ds((2 * second + which) * pad, pad)] = total[
                at * per_class : (at + 1) * per_class
            ]

    unroll = 8

    def gather(i):
        for j in range(unroll):
            pair = pair_ref[i * unroll + j]
            row = (pair & (blocks - 1)) * per_class + (pair >> (blocks.bit_length() - 1))
            s2[pl.ds(i * unroll + j, 1), :] = g[pl.ds(row, 1), :]

    loop(0, waves // 2 // unroll, gather)

    def block_of(index):
        return pl.ds(pl.multiple_of(index * slots, 8), slots)

    def copy2(k, incoming):
        peer = lax.rem(me + k, blocks)
        return pltpu.make_async_remote_copy(
            src_ref=s2.at[block_of(peer)], dst_ref=r2.at[block_of(peer if incoming else me)],
            send_sem=s2_send.at[peer], recv_sem=s2_recv.at[peer if incoming else me],
            device_id=(peer, lat), device_id_type=MESH,
        )

    loop(1, blocks, lambda k: copy2(k, False).start())
    r2[block_of(me), :] = s2[block_of(me), :]
    loop(1, blocks, lambda k: copy2(k, True).wait_recv())

    def legendre(s):
        x = r2[pl.ds(s, blocks, stride=slots), :]
        turned = [x] + [pltpu.roll(x, shift=pad * k, axis=1) for k in range(1, 4)]
        high = [t.astype(BF16).astype(F32) for t in turned]
        low = [t - h for t, h in zip(turned, high)]
        lane = lax.broadcasted_iota(jnp.int32, x.shape, 1)
        operand = jnp.concatenate(
            [
                jnp.where(lane < pad, high[-q % 4], jnp.where(lane < 2 * pad, low[(1 - q) % 4], high[(2 - q) % 4]))
                for q in range(4)
            ],
            axis=0,
        ).astype(BF16)[:, : 3 * pad]
        pair = pair_ref[me * slots + s]
        step = 2 * cw
        for n in range(0, waves + cw, step):
            size = min(step, waves + cw - n)
            sums = jnp.dot(operand, cat[s, :, pl.ds(n, size)], preferred_element_type=F32)
            for k in range(size // cw):
                column = n + k * cw + lax.broadcasted_iota(jnp.int32, (levels, cw), 1)
                if n + k * cw == waves:
                    column = jnp.full((levels, cw), waves, jnp.int32)
                second = column >= waves - pair
                odd = (jnp.where(second, column + pair, column) & 1) == 1
                chosen = []
                for r in range(2):
                    pick = [
                        sums[(2 * w + r) * 2 * levels + p * levels :][:levels, k * cw : (k + 1) * cw]
                        for w in range(2)
                        for p in range(2)
                    ]
                    chosen.append(
                        jnp.where(second, jnp.where(odd, pick[3], pick[2]), jnp.where(odd, pick[1], pick[0]))
                    )
                if n + k * cw == waves:
                    side = lax.broadcasted_iota(jnp.int32, (levels, cw), 1) < cw // 2
                    part[s, pl.ds(main_rows, levels), :] = jnp.where(side, chosen[0], chosen[1])
                else:
                    for r in range(2):
                        row = (r * tiles + n // cw + k) * levels
                        part[s, pl.ds(row, levels), :] = chosen[r]

    def sib_copy(owner):
        return pltpu.make_async_remote_copy(
            src_ref=part.at[2 * owner + other], dst_ref=sib.at[owner], send_sem=sib_send.at[owner],
            recv_sem=sib_recv.at[owner], device_id=sibling, device_id_type=MESH,
        )

    def prepare(owner):
        legendre(2 * owner + other)
        sib_copy(owner).start()
        legendre(2 * owner + core)

    def ring_copy(way, t, p):
        low, rows, _ = pieces[p]
        slot = 2 * (at_z(hops - t) if way == 0 else at_z(t - hops)) + core
        return pltpu.make_async_remote_copy(
            src_ref=part.at[slot, pl.ds(low, rows)], dst_ref=ring.at[way, t, pl.ds(low, rows)],
            send_sem=rs_send.at[way, t, p], recv_sem=rs_recv.at[way, t, p],
            device_id=z_device(1 if way == 0 else -1), device_id_type=MESH,
        )

    def first_step(way, p):
        reach = pieces[p][2] if way == 0 else depth - 1 - pieces[p][2]
        return hops - reach

    def pass_on(way, t, p, received):
        low, rows, _ = pieces[p]
        owner = at_z(hops - t) if way == 0 else at_z(t - hops)
        value = part[2 * owner + core, pl.ds(low, rows), :] + sib[owner, pl.ds(low, rows), :]
        if received:
            ring_copy(way, t - 1, p).wait_recv()
            value = value + ring[way, t - 1, pl.ds(low, rows), :]
        part[2 * owner + core, pl.ds(low, rows), :] = value
        ring_copy(way, t, p).start()

    def prepare_step(t):
        for offset in sorted({hops - t, t - hops} if t else {hops}):
            prepare(at_z(offset))

    prepare_step(0)
    prepare_step(1)
    sib_copy_wait = lambda owner: sib_copy(owner).wait_recv()

    def reduce_step(t, begun):
        sib_copy_wait(at_z(hops - t))
        if begun > 0:
            sib_copy_wait(at_z(t - hops))
        for p in range(2):
            for way in range(2):
                first = first_step(way, p)
                if begun >= first:
                    pass_on(way, t, p, begun > first)

    reduce_step(0, 0)
    prepare_step(2)
    reduce_step(1, 1)

    def middle(t):
        prepare(at_z(hops - 1 - t))
        prepare(at_z(t + 1 - hops))
        reduce_step(t, 2)

    if hops > 2:
        loop(2, hops - 1, middle)
        prepare_step(hops)
        reduce_step(hops - 1, 2)

    mine = 2 * z + core
    sib_copy_wait(z)
    pair = pair_ref[me * slots + mine]
    level_of = lax.broadcasted_iota(jnp.int32, (levels, cw), 0)
    strength = jnp.zeros((levels, cw), F32)
    for level in range(levels):
        strength = jnp.where(level_of == level, diff_ref[level], strength)

    def damping(column):
        degree = jnp.where(column >= waves - pair, column - 1, pair + column).astype(F32)
        ratio = degree * (degree + 1.0) / float((waves - 1) * waves)
        return 1.0 / (1.0 + strength * (ratio * ratio))

    def ag_copy(way, u, p):
        low, rows, _ = pieces[p]
        slot = 2 * at_z(-u if way == 0 else u) + core
        return pltpu.make_async_remote_copy(
            src_ref=final.at[slot, pl.ds(low, rows)], dst_ref=final.at[slot, pl.ds(low, rows)],
            send_sem=ag_send.at[way, u, p], recv_sem=ag_recv.at[way, u, p],
            device_id=z_device(1 if way == 0 else -1), device_id_type=MESH,
        )

    def as_copy(owner, p, side):
        low, rows, _ = pieces[p]
        slot = 2 * owner + side
        return pltpu.make_async_remote_copy(
            src_ref=final.at[slot, pl.ds(low, rows)], dst_ref=final.at[slot, pl.ds(low, rows)],
            send_sem=as_send.at[owner, p], recv_sem=as_recv.at[owner, p],
            device_id=sibling, device_id_type=MESH,
        )

    def reach(way, p):
        return pieces[p][2] if way == 0 else depth - 1 - pieces[p][2]

    for p in range(2):
        low, rows, _ = pieces[p]
        for way in range(2):
            ring_copy(way, hops - 1, p).wait_recv()
        for row in range(low, low + rows, levels):
            piece = pl.ds(row, levels)
            value = part[mine, piece, :] + sib[z, piece, :]
            value = value + ring[0, hops - 1, piece, :] + ring[1, hops - 1, piece, :]
            if row >= main_rows:
                column = jnp.full((levels, cw), waves, jnp.int32)
            else:
                first = (row // levels) % tiles * cw
                column = first + lax.broadcasted_iota(jnp.int32, (levels, cw), 1)
            final[mine, piece, :] = value * damping(column)
        for way in range(2):
            ag_copy(way, 0, p).start()
        as_copy(z, p, core).start()

    def spread(u, last):
        for p in range(2):
            for way in range(2):
                if last and reach(way, p) < hops:
                    continue
                ag_copy(way, u, p).wait_recv()
                if not last:
                    if reach(way, p) == hops:
                        ag_copy(way, u + 1, p).start()
                    else:

                        @pl.when(u + 1 < hops - 1)
                        def _():
                            ag_copy(way, u + 1, p).start()

                as_copy(at_z(-u - 1 if way == 0 else u + 1), p, core).start()

    loop(0, hops - 1, lambda u: spread(u, False))
    spread(hops - 1, True)

    def settle_owner(owner):
        sib_copy(owner).wait_send()
        for p in range(2):
            as_copy(owner, p, core).wait_send()
            as_copy(owner, p, other).wait_recv()

    loop(0, depth, settle_owner)
    whole = pltpu.make_async_copy(final, out_hbm, out_sem)
    whole.start()

    def settle_peer(k):
        send1(k).wait_send()
        copy2(k, False).wait_send()

    loop(1, blocks, settle_peer)
    for way in range(2):
        for p in range(2):
            count = reach(way, p)
            loop(hops - count, hops, lambda t: ring_copy(way, t, p).wait_send())
            loop(0, count, lambda u: ag_copy(way, u, p).wait_send())
    whole.wait()


def per_device(depth, vorticity, legendre_table, pair_slots, diffusion):
    levels, _, band, width = vorticity.shape
    slots, columns = legendre_table.shape[1:]
    blocks = lax.axis_size("lon")
    waves = columns - 1
    cw = min(128, waves)
    half, hops, tiles, pad = blocks // 2, depth // 2, waves // cw, 32
    rows = 2 * tiles * levels + levels
    dims = (blocks, depth, levels, band, width, slots, waves, cw)
    twid = jnp.asarray(twiddles(blocks, width, waves))
    dma = pltpu.SemaphoreType.DMA
    any_spec, smem = pl.BlockSpec(memory_space=pltpu.HBM), pl.BlockSpec(memory_space=pltpu.SMEM)
    raw = pl.pallas_call(
        functools.partial(kernel, dims),
        out_shape=jax.ShapeDtypeStruct((slots, rows, cw), F32),
        in_specs=[smem, smem, any_spec, any_spec, any_spec],
        out_specs=any_spec,
        scratch_shapes=[
            pltpu.VMEM((2 * levels * band, width), F32),
            pltpu.VMEM((tiles + 1, (band + 1) * slots, cw), F32),
            pltpu.VMEM((band * slots, 1), F32),
            pltpu.VMEM(twid.shape, F32),
            pltpu.VMEM((2, *twid.shape), BF16),
            pltpu.VMEM((slots, 3 * pad, waves + cw), BF16),
            pltpu.VMEM((blocks, band, width), F32),
            pltpu.VMEM((blocks, band, width), F32),
            pltpu.VMEM((waves // 2, 4 * pad), F32),
            pltpu.VMEM((waves // 2, 4 * pad), F32),
            pltpu.VMEM((waves // 2 + slots, 4 * pad), F32),
            pltpu.VMEM((slots, rows, cw), F32),
            pltpu.VMEM((depth, rows, cw), F32),
            pltpu.VMEM((2, hops, rows, cw), F32),
            pltpu.VMEM((slots, rows, cw), F32),
            dma((2,)),
            dma((tiles + 1,)),
            dma,
            dma((blocks,)),
            dma((blocks,)),
            dma((blocks,)),
            dma((blocks,)),
            dma((depth,)),
            dma((depth,)),
            dma((2, hops, 2)),
            dma((2, hops, 2)),
            dma((2, hops, 2)),
            dma((2, hops, 2)),
            dma((depth, 2)),
            dma((depth, 2)),
        ],
        compiler_params=pltpu.CompilerParams(
            collective_id=0, has_side_effects=True, vmem_limit_bytes=61 * 1024 * 1024
        ),
    )(
        pair_slots,
        diffusion,
        vorticity.reshape(2 * levels * band, width),
        legendre_table.reshape(band * slots, columns),
        twid,
    )
    main = raw[:, : 2 * tiles * levels].reshape(slots, 2, tiles, levels, cw)
    main = main.transpose(0, 3, 1, 2, 4).reshape(slots, levels, 2, waves)
    tail = raw[:, 2 * tiles * levels :]
    tail = jnp.stack([tail[:, :, 0:1], tail[:, :, cw // 2 : cw // 2 + 1]], axis=2)
    return jnp.concatenate([main, tail], axis=3)


def solution(mesh):
    placed = (P(None, None, "lat", "lon"), P("lat", "lon", None), P(), P())
    return jax.shard_map(
        functools.partial(per_device, mesh.shape["lat"] // 2),
        mesh=mesh,
        in_specs=placed,
        out_specs=P("lon", None, None, None),
        check_vma=False,
    )
```

```python
import functools
import math

import jax
import jax.numpy as jnp
import numpy as np
from jax import lax
from jax.experimental import pallas as pl
from jax.experimental.pallas import tpu as pltpu
from jax.sharding import PartitionSpec as P

MESH = pl.DeviceIdType.MESH
F32 = jnp.float32
BF16 = jnp.bfloat16


def real_dft(parts):
    n = len(parts)
    if n == 1:
        return [(parts[0], None)]
    even, odd = real_dft(parts[0::2]), real_dft(parts[1::2])
    out = [None] * (n // 2 + 1)
    for k in range(n // 4 + 1):
        er, ei = even[k]
        orr, oi = odd[k]
        if k == 0:
            out[0] = (er + orr, None)
            out[n // 2] = (er - orr, None)
        elif 4 * k == n:
            out[k] = (er, -orr)
        else:
            c, s = math.cos(2 * math.pi * k / n), math.sin(2 * math.pi * k / n)
            tr, ti = c * orr, -s * orr
            if oi is not None:
                tr, ti = tr + s * oi, ti + c * oi
            ei = 0.0 if ei is None else ei
            out[k] = (er + tr, ei + ti)
            out[n // 2 - k] = (er - tr, ti - ei)
    return out


def class_blocks(k, blocks):
    rows = [(0, k, 0, 0), (0, k, 1, 0), (1, blocks - 1 - k, 0, 0), (1, blocks - 1 - k, 1, 0)]
    if 0 < k < blocks // 2:
        rows += [(0, blocks - k, 0, 1), (0, blocks - k, 1, 1), (1, k - 1, 0, 1), (1, k - 1, 1, 1)]
    return rows


def twiddles(blocks, width, waves):
    full = blocks * width
    per_class = waves // 2 // blocks
    half = blocks // 2
    table = np.zeros((2 * half, 8 * per_class, width))
    position = np.arange(width)
    for k in range(half + 1):
        for at, (second, residue, part, conj) in enumerate(class_blocks(k, blocks)):
            pair = np.arange(per_class) * blocks + residue
            wave = waves - 1 - pair if second else pair
            angle = 2 * np.pi * ((wave[:, None] * position[None, :]) % full) / full
            cos, sin = np.cos(angle) / math.sqrt(full), np.sin(angle) / math.sqrt(full)
            sign = -1.0 if conj else 1.0
            rows = slice(at * per_class, (at + 1) * per_class)
            table[k, rows] = -sin if part else cos
            if 0 < k < half:
                table[half + k, rows] = sign * (cos if part else sin)
    return table.astype(np.float32)


def split(values):
    high = values.astype(BF16)
    return high, (values - high.astype(F32)).astype(BF16)


def dot_t(a, b):
    return lax.dot_general(a, b, (((1,), (1,)), ((), ())), preferred_element_type=F32)


def kernel(
    dims, pair_ref, diff_ref, vort_hbm, table_hbm, twid_hbm, out_hbm,
    vort, table, tail, twid, twid_split, cat, s1, r1, g, s2, r2, part, sib, ring, final, spread,
    load_sem, tab_sem, out_sem, s1_send, s1_recv, s2_send, s2_recv, sib_send, sib_recv,
    rs_send, rs_recv, ag_send, ag_recv, as_send, as_recv,
):
    blocks, depth, levels, band, width, slots, waves, cw = dims
    half, hops = blocks // 2, depth // 2
    tiles = waves // cw
    pad = 32
    per_class = waves // 2 // blocks
    main_rows = 2 * tiles * levels
    pieces = ((0, main_rows // 2, hops), (main_rows // 2, main_rows // 2 + levels, hops - 1))

    meet = [c for c in (0, 1, 2, 4, 6) if c < hops]

    def parent(d):
        return max(c for c in meet if c < d)

    def children(c):
        return sorted((d for d in range(1, hops + 1) if parent(d) == c), reverse=True)

    me = lax.axis_index("lon")
    lat = lax.axis_index("lat")
    z, core = lat // 2, lat % 2
    other = 1 - core

    def at_z(step):
        return lax.rem(z + step + depth, depth)

    def z_device(step):
        return (me, at_z(step) * 2 + core)

    sibling = (me, z * 2 + other)

    load = pltpu.make_async_copy(vort_hbm, vort, load_sem.at[0])
    load.start()
    load_twid = pltpu.make_async_copy(twid_hbm, twid, load_sem.at[1])
    load_twid.start()

    def table_copy(k):
        if k == tiles:
            return pltpu.make_async_copy(table_hbm.at[:, pl.ds(waves, 1)], tail, tab_sem.at[k])
        return pltpu.make_async_copy(
            table_hbm.at[:, pl.ds(k * cw, cw)], table.at[k, pl.ds(0, band * slots)], tab_sem.at[k]
        )

    for k in range(tiles + 1):
        table_copy(k).start()

    barrier = pltpu.get_barrier_semaphore()

    def greet(k, carry):
        peer = lax.rem(me + k, blocks)
        pl.semaphore_signal(barrier, inc=1, device_id=(peer, lat), device_id_type=MESH)
        return carry

    lax.fori_loop(1, blocks, greet, 0)
    near = sorted({sign * (d - parent(d)) for d in range(1, hops + 1) for sign in (1, -1)})
    for target in [z_device(step) for step in near] + [sibling]:
        pl.semaphore_signal(barrier, inc=1, device_id=target, device_id_type=MESH)

    load.wait()
    for level in range(levels):
        north = vort[pl.ds(2 * level * band, band), :]
        south = vort[pl.ds((2 * level + 1) * band, band), :]
        s1[level] = north + south
        s1[levels + level] = north - south

    pl.semaphore_wait(barrier, blocks + len(near))

    def send1(k):
        peer = lax.rem(me + k, blocks)
        return pltpu.make_async_remote_copy(
            src_ref=s1.at[peer], dst_ref=r1.at[me], send_sem=s1_send.at[peer],
            recv_sem=s1_recv.at[me], device_id=(peer, lat), device_id_type=MESH,
        )

    def recv1(k):
        peer = lax.rem(me + k, blocks)
        return pltpu.make_async_remote_copy(
            src_ref=s1.at[peer], dst_ref=r1.at[peer], send_sem=s1_send.at[peer],
            recv_sem=s1_recv.at[peer], device_id=(peer, lat), device_id_type=MESH,
        )

    def loop(low, high, body):
        def step(k, carry):
            body(k)
            return carry

        lax.fori_loop(low, high, step, 0)

    loop(1, blocks, lambda k: send1(k).start())
    r1[me] = s1[me]

    for k in range(tiles + 1):
        table_copy(k).wait()
    table[tiles, pl.ds(0, band * slots), :] = jnp.broadcast_to(tail[...], (band * slots, cw))

    def stack_table(s):
        for k in range(tiles + 1):
            rows = table[k, pl.ds(s, band, stride=slots), :]
            if band < pad:
                rows = jnp.concatenate([rows, jnp.zeros((pad - band, cw), F32)], axis=0)
            high, low = split(rows)
            lanes = pl.ds(k * cw, cw)
            cat[s, pl.ds(0, pad), lanes] = high
            cat[s, pl.ds(pad, pad), lanes] = high
            cat[s, pl.ds(2 * pad, pad), lanes] = low

    loop(0, slots, stack_table)

    load_twid.wait()

    def split_twiddles(k):
        high, low = split(twid[k])
        twid_split[0, k] = high
        twid_split[1, k] = low

    loop(0, 2 * half, split_twiddles)
    loop(1, blocks, lambda k: recv1(k).wait_recv())

    spectrum = real_dft([r1[a] for a in range(blocks)])
    for k in range(half + 1):
        rows = class_blocks(k, blocks)
        count = len(rows) * per_class
        total = None
        for number, value in ((k, spectrum[k][0]), (half + k, spectrum[k][1])):
            if value is None:
                continue
            if band < pad:
                value = jnp.concatenate([value, jnp.zeros((pad - band, width), F32)], axis=0)
            high, low = split(value)
            w_high = twid_split[0, number, pl.ds(0, count), :]
            w_low = twid_split[1, number, pl.ds(0, count), :]
            term = dot_t(w_high, high) + (dot_t(w_high, low) + dot_t(w_low, high))
            total = term if total is None else total + term
        for at, (second, residue, which, _) in enumerate(rows):
            g[pl.ds(residue * per_class, per_class), pl.ds((2 * second + which) * pad, pad)] = total[
                at * per_class : (at + 1) * per_class
            ]

    unroll = 8

    def gather(i):
        for j in range(unroll):
            pair = pair_ref[i * unroll + j]
            row = (pair & (blocks - 1)) * per_class + (pair >> (blocks.bit_length() - 1))
            s2[pl.ds(i * unroll + j, 1), :] = g[pl.ds(row, 1), :]

    loop(0, waves // 2 // unroll, gather)

    def block_of(index):
        return pl.ds(pl.multiple_of(index * slots, 8), slots)

    def copy2(k, incoming):
        peer = lax.rem(me + k, blocks)
        return pltpu.make_async_remote_copy(
            src_ref=s2.at[block_of(peer)], dst_ref=r2.at[block_of(peer if incoming else me)],
            send_sem=s2_send.at[peer], recv_sem=s2_recv.at[peer if incoming else me],
            device_id=(peer, lat), device_id_type=MESH,
        )

    loop(1, blocks, lambda k: copy2(k, False).start())
    r2[block_of(me), :] = s2[block_of(me), :]
    loop(1, blocks, lambda k: copy2(k, True).wait_recv())

    def legendre(s):
        x = r2[pl.ds(s, blocks, stride=slots), :]
        turned = [x] + [pltpu.roll(x, shift=pad * k, axis=1) for k in range(1, 4)]
        high = [t.astype(BF16).astype(F32) for t in turned]
        low = [t - h for t, h in zip(turned, high)]
        lane = lax.broadcasted_iota(jnp.int32, x.shape, 1)
        operand = jnp.concatenate(
            [
                jnp.where(lane < pad, high[-q % 4], jnp.where(lane < 2 * pad, low[(1 - q) % 4], high[(2 - q) % 4]))
                for q in range(4)
            ],
            axis=0,
        ).astype(BF16)[:, : 3 * pad]
        pair = pair_ref[me * slots + s]
        step = 2 * cw
        for n in range(0, waves + cw, step):
            size = min(step, waves + cw - n)
            sums = jnp.dot(operand, cat[s, :, pl.ds(n, size)], preferred_element_type=F32)
            for k in range(size // cw):
                column = n + k * cw + lax.broadcasted_iota(jnp.int32, (levels, cw), 1)
                if n + k * cw == waves:
                    column = jnp.full((levels, cw), waves, jnp.int32)
                second = column >= waves - pair
                odd = (jnp.where(second, column + pair, column) & 1) == 1
                chosen = []
                for r in range(2):
                    pick = [
                        sums[(2 * w + r) * 2 * levels + p * levels :][:levels, k * cw : (k + 1) * cw]
                        for w in range(2)
                        for p in range(2)
                    ]
                    chosen.append(
                        jnp.where(second, jnp.where(odd, pick[3], pick[2]), jnp.where(odd, pick[1], pick[0]))
                    )
                if n + k * cw == waves:
                    side = lax.broadcasted_iota(jnp.int32, (levels, cw), 1) < cw // 2
                    part[s, pl.ds(main_rows, levels), :] = jnp.where(side, chosen[0], chosen[1])
                else:
                    for r in range(2):
                        row = (r * tiles + n // cw + k) * levels
                        part[s, pl.ds(row, levels), :] = chosen[r]

    def sib_copy(owner):
        return pltpu.make_async_remote_copy(
            src_ref=part.at[2 * owner + other], dst_ref=sib.at[owner], send_sem=sib_send.at[owner],
            recv_sem=sib_recv.at[owner], device_id=sibling, device_id_type=MESH,
        )

    def owner_at(way, d):
        return at_z(d if way == 0 else -d)

    def reach(way, p):
        return pieces[p][2] if way == 0 else depth - 1 - pieces[p][2]

    def prepare(d):
        count = 2 if 0 < d < hops else 1

        def one(i):
            sign = 1 - 2 * lax.rem(i, count)
            owner = at_z(sign * d)
            away = i < count
            slot = 2 * owner + jnp.where(away, other, core)
            legendre(slot)

            @pl.when(away)
            def _():
                sib_copy(owner).start()

        loop(0, 2 * count, one)

    def ring_copy(way, d, p):
        low, rows, _ = pieces[p]
        slot = 2 * owner_at(way, d) + core
        hop = d - parent(d)
        return pltpu.make_async_remote_copy(
            src_ref=part.at[slot, pl.ds(low, rows)], dst_ref=ring.at[way, d - 1, pl.ds(low, rows)],
            send_sem=rs_send.at[way, d - 1, p], recv_sem=rs_recv.at[way, d - 1, p],
            device_id=z_device(hop if way == 0 else -hop), device_id_type=MESH,
        )

    def pass_on(d):
        sib_copy(owner_at(0, d)).wait_recv()
        if d < hops:
            sib_copy(owner_at(1, d)).wait_recv()
        for p in range(2):
            low, rows, _ = pieces[p]
            for way in range(2):
                if d > reach(way, p):
                    continue
                owner = owner_at(way, d)
                value = part[2 * owner + core, pl.ds(low, rows), :] + sib[owner, pl.ds(low, rows), :]
                for child in children(d) if d in meet else ():
                    if child <= reach(way, p):
                        ring_copy(way, child, p).wait_recv()
                        value = value + ring[way, child - 1, pl.ds(low, rows), :]
                part[2 * owner + core, pl.ds(low, rows), :] = value
                ring_copy(way, d, p).start()

    waiting = []
    for d in range(hops, -1, -1):
        prepare(d)
        for late in list(waiting):
            if late not in meet or not children(late) or late - d >= 2 or d == 0:
                pass_on(late)
                waiting.remove(late)
        if d:
            waiting.append(d)

    mine = 2 * z + core
    sib_copy(z).wait_recv()
    pair = pair_ref[me * slots + mine]
    level_of = lax.broadcasted_iota(jnp.int32, (levels, cw), 0)
    strength = jnp.zeros((levels, cw), F32)
    for level in range(levels):
        strength = jnp.where(level_of == level, diff_ref[level], strength)

    def damping(column):
        degree = jnp.where(column >= waves - pair, column - 1, pair + column).astype(F32)
        ratio = degree * (degree + 1.0) / float((waves - 1) * waves)
        return 1.0 / (1.0 + strength * (ratio * ratio))

    def ag_copy(way, d, p):
        low, rows, _ = pieces[p]
        hop = d - parent(d)
        slot = 2 * owner_at(1 - way, parent(d)) + core
        return pltpu.make_async_remote_copy(
            src_ref=final.at[slot, pl.ds(low, rows)], dst_ref=final.at[slot, pl.ds(low, rows)],
            send_sem=ag_send.at[way, d - 1, p], recv_sem=ag_recv.at[way, d - 1, p],
            device_id=z_device(hop if way == 0 else -hop), device_id_type=MESH,
        )

    def as_copy(owner, p, side):
        low, rows, _ = pieces[p]
        slot = 2 * owner + side
        return pltpu.make_async_remote_copy(
            src_ref=final.at[slot, pl.ds(low, rows)], dst_ref=final.at[slot, pl.ds(low, rows)],
            send_sem=as_send.at[owner, p], recv_sem=as_recv.at[owner, p],
            device_id=sibling, device_id_type=MESH,
        )

    def go_on(way, d, p):
        for child in children(d) if d in meet else ():
            if child <= reach(way, p):
                ag_copy(way, child, p).start()

    def lay_out(slot, p):
        low, rows, _ = pieces[p]
        for k in range(tiles):
            spread[slot, :, p, pl.ds(k * cw, cw)] = final[slot, pl.ds(low + k * levels, levels), :]
        if p:
            last = final[slot, pl.ds(main_rows, levels), :]
            spread[slot, :, 0, pl.ds(waves, 1)] = last[:, 0:1]
            spread[slot, :, 1, pl.ds(waves, 1)] = last[:, cw // 2 : cw // 2 + 1]

    def out_copy(slot):
        return pltpu.make_async_copy(spread.at[slot], out_hbm.at[slot], out_sem.at[slot])

    for p in range(2):
        low, rows, _ = pieces[p]
        for way in range(2):
            for child in children(0):
                ring_copy(way, child, p).wait_recv()
        for row in range(low, low + rows, levels):
            piece = pl.ds(row, levels)
            value = part[mine, piece, :] + sib[z, piece, :]
            for way in range(2):
                for child in children(0):
                    value = value + ring[way, child - 1, piece, :]
            if row >= main_rows:
                column = jnp.full((levels, cw), waves, jnp.int32)
            else:
                first = (row // levels) % tiles * cw
                column = first + lax.broadcasted_iota(jnp.int32, (levels, cw), 1)
            final[mine, piece, :] = value * damping(column)
        for way in range(2):
            go_on(way, 0, p)
        as_copy(z, p, core).start()

    def finish(d):
        for way in range(2 if 0 < d < hops else 1):
            owner = owner_at(way, d)
            for p in range(2):
                as_copy(owner, p, other).wait_recv()
                lay_out(2 * owner + core, p)
                lay_out(2 * owner + other, p)
            out_copy(2 * owner + core).start()
            out_copy(2 * owner + other).start()

    done = [0]
    order = sorted(range(1, hops + 1), key=lambda d: d - 1.5 * (d in meet and bool(children(d)) or d == hops))
    for d in order:
        for p in range(2):
            for way in range(2):
                if d <= reach(way, p):
                    ag_copy(way, d, p).wait_recv()
                    go_on(way, d, p)
                    as_copy(owner_at(1 - way, d), p, core).start()
        finish(done[-1])
        done.append(d)
    finish(done[-1])

    def settle_owner(owner):
        sib_copy(owner).wait_send()
        for p in range(2):
            as_copy(owner, p, core).wait_send()

    loop(0, depth, settle_owner)

    def settle_peer(k):
        send1(k).wait_send()
        copy2(k, False).wait_send()

    loop(1, blocks, settle_peer)
    for way in range(2):
        for p in range(2):
            for d in range(1, reach(way, p) + 1):
                ring_copy(way, d, p).wait_send()
                ag_copy(way, d, p).wait_send()
    loop(0, slots, lambda slot: out_copy(slot).wait())


def per_device(depth, vorticity, legendre_table, pair_slots, diffusion):
    levels, _, band, width = vorticity.shape
    slots, columns = legendre_table.shape[1:]
    blocks = lax.axis_size("lon")
    waves = columns - 1
    cw = min(128, waves)
    half, hops, tiles, pad = blocks // 2, depth // 2, waves // cw, 32
    rows = 2 * tiles * levels + levels
    dims = (blocks, depth, levels, band, width, slots, waves, cw)
    twid = jnp.asarray(twiddles(blocks, width, waves))
    dma = pltpu.SemaphoreType.DMA
    any_spec, smem = pl.BlockSpec(memory_space=pltpu.HBM), pl.BlockSpec(memory_space=pltpu.SMEM)
    return pl.pallas_call(
        functools.partial(kernel, dims),
        out_shape=jax.ShapeDtypeStruct((slots, levels, 2, columns), F32),
        in_specs=[smem, smem, any_spec, any_spec, any_spec],
        out_specs=any_spec,
        scratch_shapes=[
            pltpu.VMEM((2 * levels * band, width), F32),
            pltpu.VMEM((tiles + 1, (band + 1) * slots, cw), F32),
            pltpu.VMEM((band * slots, 1), F32),
            pltpu.VMEM(twid.shape, F32),
            pltpu.VMEM((2, *twid.shape), BF16),
            pltpu.VMEM((slots, 3 * pad, waves + cw), BF16),
            pltpu.VMEM((blocks, band, width), F32),
            pltpu.VMEM((blocks, band, width), F32),
            pltpu.VMEM((waves // 2, 4 * pad), F32),
            pltpu.VMEM((waves // 2, 4 * pad), F32),
            pltpu.VMEM((waves // 2 + slots, 4 * pad), F32),
            pltpu.VMEM((slots, rows, cw), F32),
            pltpu.VMEM((depth, rows, cw), F32),
            pltpu.VMEM((2, hops, rows, cw), F32),
            pltpu.VMEM((slots, rows, cw), F32),
            pltpu.VMEM((slots, levels, 2, columns), F32),
            dma((2,)),
            dma((tiles + 1,)),
            dma((slots,)),
            dma((blocks,)),
            dma((blocks,)),
            dma((blocks,)),
            dma((blocks,)),
            dma((depth,)),
            dma((depth,)),
            dma((2, hops, 2)),
            dma((2, hops, 2)),
            dma((2, hops, 2)),
            dma((2, hops, 2)),
            dma((depth, 2)),
            dma((depth, 2)),
        ],
        compiler_params=pltpu.CompilerParams(
            collective_id=0, has_side_effects=True, vmem_limit_bytes=61 * 1024 * 1024
        ),
    )(
        pair_slots,
        diffusion,
        vorticity.reshape(2 * levels * band, width),
        legendre_table.reshape(band * slots, columns),
        twid,
    )


def solution(mesh):
    placed = (P(None, None, "lat", "lon"), P("lat", "lon", None), P(), P())
    return jax.shard_map(
        functools.partial(per_device, mesh.shape["lat"] // 2),
        mesh=mesh,
        in_specs=placed,
        out_specs=P("lon", None, None, None),
        check_vma=False,
    )
```

```python
import functools
import math

import jax
import jax.numpy as jnp
import numpy as np
from jax import lax
from jax.experimental import pallas as pl
from jax.experimental.pallas import tpu as pltpu
from jax.sharding import PartitionSpec as P

MESH = pl.DeviceIdType.MESH
CUTS = 1
MEET = (0, 1, 2, 4, 6)
F32 = jnp.float32
BF16 = jnp.bfloat16


def real_dft(parts):
    n = len(parts)
    if n == 1:
        return [(parts[0], None)]
    even, odd = real_dft(parts[0::2]), real_dft(parts[1::2])
    out = [None] * (n // 2 + 1)
    for k in range(n // 4 + 1):
        er, ei = even[k]
        orr, oi = odd[k]
        if k == 0:
            out[0] = (er + orr, None)
            out[n // 2] = (er - orr, None)
        elif 4 * k == n:
            out[k] = (er, -orr)
        else:
            c, s = math.cos(2 * math.pi * k / n), math.sin(2 * math.pi * k / n)
            tr, ti = c * orr, -s * orr
            if oi is not None:
                tr, ti = tr + s * oi, ti + c * oi
            ei = 0.0 if ei is None else ei
            out[k] = (er + tr, ei + ti)
            out[n // 2 - k] = (er - tr, ti - ei)
    return out


def class_blocks(k, blocks):
    rows = [(0, k, 0, 0), (0, k, 1, 0), (1, blocks - 1 - k, 0, 0), (1, blocks - 1 - k, 1, 0)]
    if 0 < k < blocks // 2:
        rows += [(0, blocks - k, 0, 1), (0, blocks - k, 1, 1), (1, k - 1, 0, 1), (1, k - 1, 1, 1)]
    return rows


def twiddles(blocks, width, waves):
    full = blocks * width
    per_class = waves // 2 // blocks
    half = blocks // 2
    table = np.zeros((2 * half, 8 * per_class, width))
    position = np.arange(width)
    for k in range(half + 1):
        for at, (second, residue, part, conj) in enumerate(class_blocks(k, blocks)):
            pair = np.arange(per_class) * blocks + residue
            wave = waves - 1 - pair if second else pair
            angle = 2 * np.pi * ((wave[:, None] * position[None, :]) % full) / full
            cos, sin = np.cos(angle) / math.sqrt(full), np.sin(angle) / math.sqrt(full)
            sign = -1.0 if conj else 1.0
            rows = slice(at * per_class, (at + 1) * per_class)
            table[k, rows] = -sin if part else cos
            if 0 < k < half:
                table[half + k, rows] = sign * (cos if part else sin)
    return table.astype(np.float32)


def split(values):
    high = values.astype(BF16)
    return high, (values - high.astype(F32)).astype(BF16)


def dot_t(a, b):
    return lax.dot_general(a, b, (((1,), (1,)), ((), ())), preferred_element_type=F32)


def kernel(
    dims, pair_ref, diff_ref, vort_hbm, table_hbm, twid_hbm, out_hbm,
    vort, table, tail, twid, twid_split, cat, s1, r1, g, s2, r2, part, sib, ring, final, spread,
    load_sem, tab_sem, out_sem, s1_send, s1_recv, s2_send, s2_recv, sib_send, sib_recv,
    rs_send, rs_recv, ag_send, ag_recv, as_send, as_recv,
):
    blocks, depth, levels, band, width, slots, waves, cw = dims
    half, hops = blocks // 2, depth // 2
    tiles = waves // cw
    pad = 32
    per_class = waves // 2 // blocks
    main_rows = 2 * tiles * levels
    cut = min(CUTS, tiles)
    size = main_rows // 2 // cut
    pieces = [(k * size, size, hops - k // cut) for k in range(2 * cut)]
    pieces[-1] = (pieces[-1][0], size + levels, hops - 1)

    meet = [c for c in MEET if c < hops]

    def parent(d):
        return max(c for c in meet if c < d)

    def children(c):
        return sorted((d for d in range(1, hops + 1) if parent(d) == c), reverse=True)

    me = lax.axis_index("lon")
    lat = lax.axis_index("lat")
    z, core = lat // 2, lat % 2
    other = 1 - core

    def at_z(step):
        return lax.rem(z + step + depth, depth)

    def z_device(step):
        return (me, at_z(step) * 2 + core)

    sibling = (me, z * 2 + other)

    load = pltpu.make_async_copy(vort_hbm, vort, load_sem.at[0])
    load.start()
    load_twid = pltpu.make_async_copy(twid_hbm, twid, load_sem.at[1])
    load_twid.start()

    def table_copy(k):
        if k == tiles:
            return pltpu.make_async_copy(table_hbm.at[:, pl.ds(waves, 1)], tail, tab_sem.at[k])
        return pltpu.make_async_copy(
            table_hbm.at[:, pl.ds(k * cw, cw)], table.at[k, pl.ds(0, band * slots)], tab_sem.at[k]
        )

    for k in range(tiles + 1):
        table_copy(k).start()

    barrier = pltpu.get_barrier_semaphore()

    def greet(k, carry):
        peer = lax.rem(me + k, blocks)
        pl.semaphore_signal(barrier, inc=1, device_id=(peer, lat), device_id_type=MESH)
        return carry

    lax.fori_loop(1, blocks, greet, 0)
    near = sorted({sign * (d - parent(d)) for d in range(1, hops + 1) for sign in (1, -1)})
    for target in [z_device(step) for step in near] + [sibling]:
        pl.semaphore_signal(barrier, inc=1, device_id=target, device_id_type=MESH)

    load.wait()
    for level in range(levels):
        north = vort[pl.ds(2 * level * band, band), :]
        south = vort[pl.ds((2 * level + 1) * band, band), :]
        s1[level] = north + south
        s1[levels + level] = north - south

    pl.semaphore_wait(barrier, blocks + len(near))

    def send1(k):
        peer = lax.rem(me + k, blocks)
        return pltpu.make_async_remote_copy(
            src_ref=s1.at[peer], dst_ref=r1.at[me], send_sem=s1_send.at[peer],
            recv_sem=s1_recv.at[me], device_id=(peer, lat), device_id_type=MESH,
        )

    def recv1(k):
        peer = lax.rem(me + k, blocks)
        return pltpu.make_async_remote_copy(
            src_ref=s1.at[peer], dst_ref=r1.at[peer], send_sem=s1_send.at[peer],
            recv_sem=s1_recv.at[peer], device_id=(peer, lat), device_id_type=MESH,
        )

    def loop(low, high, body):
        def step(k, carry):
            body(k)
            return carry

        lax.fori_loop(low, high, step, 0)

    loop(1, blocks, lambda k: send1(k).start())
    r1[me] = s1[me]

    for k in range(tiles + 1):
        table_copy(k).wait()
    table[tiles, pl.ds(0, band * slots), :] = jnp.broadcast_to(tail[...], (band * slots, cw))

    def stack_table(s):
        for k in range(tiles + 1):
            rows = table[k, pl.ds(s, band, stride=slots), :]
            if band < pad:
                rows = jnp.concatenate([rows, jnp.zeros((pad - band, cw), F32)], axis=0)
            high, low = split(rows)
            lanes = pl.ds(k * cw, cw)
            cat[s, pl.ds(0, pad), lanes] = high
            cat[s, pl.ds(pad, pad), lanes] = high
            cat[s, pl.ds(2 * pad, pad), lanes] = low

    load_twid.wait()

    def split_twiddles(k):
        high, low = split(twid[k])
        twid_split[0, k] = high
        twid_split[1, k] = low

    loop(0, 2 * half, split_twiddles)
    loop(0, slots * 3 // 8, stack_table)
    loop(1, blocks, lambda k: recv1(k).wait_recv())

    spectrum = real_dft([r1[a] for a in range(blocks)])
    for k in range(half + 1):
        rows = class_blocks(k, blocks)
        count = len(rows) * per_class
        total = None
        for number, value in ((k, spectrum[k][0]), (half + k, spectrum[k][1])):
            if value is None:
                continue
            if band < pad:
                value = jnp.concatenate([value, jnp.zeros((pad - band, width), F32)], axis=0)
            high, low = split(value)
            w_high = twid_split[0, number, pl.ds(0, count), :]
            w_low = twid_split[1, number, pl.ds(0, count), :]
            term = dot_t(w_high, high) + (dot_t(w_high, low) + dot_t(w_low, high))
            total = term if total is None else total + term
        for at, (second, residue, which, _) in enumerate(rows):
            g[pl.ds(residue * per_class, per_class), pl.ds((2 * second + which) * pad, pad)] = total[
                at * per_class : (at + 1) * per_class
            ]

    unroll = 8

    def gather(i):
        for j in range(unroll):
            pair = pair_ref[i * unroll + j]
            row = (pair & (blocks - 1)) * per_class + (pair >> (blocks.bit_length() - 1))
            s2[pl.ds(i * unroll + j, 1), :] = g[pl.ds(row, 1), :]

    loop(0, waves // 2 // unroll, gather)

    def block_of(index):
        return pl.ds(pl.multiple_of(index * slots, 8), slots)

    def copy2(k, incoming):
        peer = lax.rem(me + k, blocks)
        return pltpu.make_async_remote_copy(
            src_ref=s2.at[block_of(peer)], dst_ref=r2.at[block_of(peer if incoming else me)],
            send_sem=s2_send.at[peer], recv_sem=s2_recv.at[peer if incoming else me],
            device_id=(peer, lat), device_id_type=MESH,
        )

    loop(1, blocks, lambda k: copy2(k, False).start())
    r2[block_of(me), :] = s2[block_of(me), :]
    loop(slots * 3 // 8, slots, stack_table)
    loop(1, blocks, lambda k: copy2(k, True).wait_recv())

    def legendre(s):
        x = r2[pl.ds(s, blocks, stride=slots), :]
        turned = [x] + [pltpu.roll(x, shift=pad * k, axis=1) for k in range(1, 4)]
        high = [t.astype(BF16).astype(F32) for t in turned]
        low = [t - h for t, h in zip(turned, high)]
        lane = lax.broadcasted_iota(jnp.int32, x.shape, 1)
        operand = jnp.concatenate(
            [
                jnp.where(lane < pad, high[-q % 4], jnp.where(lane < 2 * pad, low[(1 - q) % 4], high[(2 - q) % 4]))
                for q in range(4)
            ],
            axis=0,
        ).astype(BF16)[:, : 3 * pad]
        pair = pair_ref[me * slots + s]
        step = 2 * cw
        for n in range(0, waves + cw, step):
            size = min(step, waves + cw - n)
            sums = jnp.dot(operand, cat[s, :, pl.ds(n, size)], preferred_element_type=F32)
            for k in range(size // cw):
                column = n + k * cw + lax.broadcasted_iota(jnp.int32, (levels, cw), 1)
                if n + k * cw == waves:
                    column = jnp.full((levels, cw), waves, jnp.int32)
                second = column >= waves - pair
                odd = (jnp.where(second, column + pair, column) & 1) == 1
                chosen = []
                for r in range(2):
                    pick = [
                        sums[(2 * w + r) * 2 * levels + p * levels :][:levels, k * cw : (k + 1) * cw]
                        for w in range(2)
                        for p in range(2)
                    ]
                    chosen.append(
                        jnp.where(second, jnp.where(odd, pick[3], pick[2]), jnp.where(odd, pick[1], pick[0]))
                    )
                if n + k * cw == waves:
                    side = lax.broadcasted_iota(jnp.int32, (levels, cw), 1) < cw // 2
                    part[s, pl.ds(main_rows, levels), :] = jnp.where(side, chosen[0], chosen[1])
                else:
                    for r in range(2):
                        row = (r * tiles + n // cw + k) * levels
                        part[s, pl.ds(row, levels), :] = chosen[r]

    def sib_copy(owner):
        return pltpu.make_async_remote_copy(
            src_ref=part.at[2 * owner + other], dst_ref=sib.at[owner], send_sem=sib_send.at[owner],
            recv_sem=sib_recv.at[owner], device_id=sibling, device_id_type=MESH,
        )

    def owner_at(way, d):
        return at_z(d if way == 0 else -d)

    def reach(way, p):
        return pieces[p][2] if way == 0 else depth - 1 - pieces[p][2]

    def prepare(d):
        count = 2 if 0 < d < hops else 1

        def one(i):
            sign = 1 - 2 * lax.rem(i, count)
            owner = at_z(sign * d)
            away = i < count
            slot = 2 * owner + jnp.where(away, other, core)
            legendre(slot)

            @pl.when(away)
            def _():
                sib_copy(owner).start()

        loop(0, 2 * count, one)

    def ring_copy(way, d, p):
        low, rows, _ = pieces[p]
        slot = 2 * owner_at(way, d) + core
        hop = d - parent(d)
        return pltpu.make_async_remote_copy(
            src_ref=part.at[slot, pl.ds(low, rows)], dst_ref=ring.at[way, d - 1, pl.ds(low, rows)],
            send_sem=rs_send.at[way, d - 1, p], recv_sem=rs_recv.at[way, d - 1, p],
            device_id=z_device(hop if way == 0 else -hop), device_id_type=MESH,
        )

    def pass_on(d):
        sib_copy(owner_at(0, d)).wait_recv()
        if d < hops:
            sib_copy(owner_at(1, d)).wait_recv()
        for p in range(len(pieces)):
            low, rows, _ = pieces[p]
            for way in range(2):
                if d > reach(way, p):
                    continue
                owner = owner_at(way, d)
                value = part[2 * owner + core, pl.ds(low, rows), :] + sib[owner, pl.ds(low, rows), :]
                for child in children(d) if d in meet else ():
                    if child <= reach(way, p):
                        ring_copy(way, child, p).wait_recv()
                        value = value + ring[way, child - 1, pl.ds(low, rows), :]
                part[2 * owner + core, pl.ds(low, rows), :] = value
                ring_copy(way, d, p).start()

    waiting = []
    for d in range(hops, -1, -1):
        prepare(d)
        for late in list(waiting):
            if late not in meet or not children(late) or late - d >= 2 or d == 0:
                pass_on(late)
                waiting.remove(late)
        if d:
            waiting.append(d)

    mine = 2 * z + core
    sib_copy(z).wait_recv()
    pair = pair_ref[me * slots + mine]
    level_of = lax.broadcasted_iota(jnp.int32, (levels, cw), 0)
    strength = jnp.zeros((levels, cw), F32)
    for level in range(levels):
        strength = jnp.where(level_of == level, diff_ref[level], strength)

    def damping(column):
        degree = jnp.where(column >= waves - pair, column - 1, pair + column).astype(F32)
        ratio = degree * (degree + 1.0) / float((waves - 1) * waves)
        return 1.0 / (1.0 + strength * (ratio * ratio))

    def ag_copy(way, d, p):
        low, rows, _ = pieces[p]
        hop = d - parent(d)
        slot = 2 * owner_at(1 - way, parent(d)) + core
        return pltpu.make_async_remote_copy(
            src_ref=final.at[slot, pl.ds(low, rows)], dst_ref=final.at[slot, pl.ds(low, rows)],
            send_sem=ag_send.at[way, d - 1, p], recv_sem=ag_recv.at[way, d - 1, p],
            device_id=z_device(hop if way == 0 else -hop), device_id_type=MESH,
        )

    def as_copy(owner, p, side):
        low, rows, _ = pieces[p]
        slot = 2 * owner + side
        return pltpu.make_async_remote_copy(
            src_ref=final.at[slot, pl.ds(low, rows)], dst_ref=final.at[slot, pl.ds(low, rows)],
            send_sem=as_send.at[owner, p], recv_sem=as_recv.at[owner, p],
            device_id=sibling, device_id_type=MESH,
        )

    def go_on(way, d, p):
        for child in children(d) if d in meet else ():
            if child <= reach(way, p):
                ag_copy(way, child, p).start()

    def lay_out(slot, p):
        low, rows, _ = pieces[p]
        for row in range(low, min(low + rows, main_rows), levels):
            k = (row // levels) % tiles
            spread[slot, :, row // (tiles * levels), pl.ds(k * cw, cw)] = final[slot, pl.ds(row, levels), :]
        if low + rows > main_rows:
            last = final[slot, pl.ds(main_rows, levels), :]
            spread[slot, :, 0, pl.ds(waves, 1)] = last[:, 0:1]
            spread[slot, :, 1, pl.ds(waves, 1)] = last[:, cw // 2 : cw // 2 + 1]

    def out_copy(slot):
        return pltpu.make_async_copy(spread.at[slot], out_hbm.at[slot], out_sem.at[slot])

    for p in range(len(pieces)):
        low, rows, _ = pieces[p]
        for way in range(2):
            for child in children(0):
                ring_copy(way, child, p).wait_recv()
        for row in range(low, low + rows, levels):
            piece = pl.ds(row, levels)
            value = part[mine, piece, :] + sib[z, piece, :]
            for way in range(2):
                for child in children(0):
                    value = value + ring[way, child - 1, piece, :]
            if row >= main_rows:
                column = jnp.full((levels, cw), waves, jnp.int32)
            else:
                first = (row // levels) % tiles * cw
                column = first + lax.broadcasted_iota(jnp.int32, (levels, cw), 1)
            final[mine, piece, :] = value * damping(column)
        for way in range(2):
            go_on(way, 0, p)
        as_copy(z, p, core).start()

    def finish(d):
        for way in range(2 if 0 < d < hops else 1):
            owner = owner_at(way, d)
            for p in range(len(pieces)):
                as_copy(owner, p, other).wait_recv()
                lay_out(2 * owner + core, p)
                lay_out(2 * owner + other, p)
            out_copy(2 * owner + core).start()
            out_copy(2 * owner + other).start()

    done = [0]
    order = sorted(range(1, hops + 1), key=lambda d: d - 1.5 * (d in meet and bool(children(d)) or d == hops))
    for d in order:
        for p in range(len(pieces)):
            for way in range(2):
                if d <= reach(way, p):
                    ag_copy(way, d, p).wait_recv()
                    go_on(way, d, p)
                    as_copy(owner_at(1 - way, d), p, core).start()
        finish(done[-1])
        done.append(d)
    finish(done[-1])

    def settle_owner(owner):
        sib_copy(owner).wait_send()
        for p in range(len(pieces)):
            as_copy(owner, p, core).wait_send()

    loop(0, depth, settle_owner)

    def settle_peer(k):
        send1(k).wait_send()
        copy2(k, False).wait_send()

    loop(1, blocks, settle_peer)
    for way in range(2):
        for p in range(len(pieces)):
            for d in range(1, reach(way, p) + 1):
                ring_copy(way, d, p).wait_send()
                ag_copy(way, d, p).wait_send()
    loop(0, slots, lambda slot: out_copy(slot).wait())


def hand_over(groups, source, target, held, in_sem, out_sem):
    size = source.shape[0] // groups
    parts = [pl.ds(k * size, size) for k in range(groups)]
    reads = [pltpu.make_async_copy(source.at[at], held.at[at], in_sem.at[k]) for k, at in enumerate(parts)]
    writes = [pltpu.make_async_copy(held.at[at], target.at[at], out_sem.at[k]) for k, at in enumerate(parts)]
    for read in reads:
        read.start()
    for read, write in zip(reads, writes):
        read.wait()
        write.start()
    for write in writes:
        write.wait()


def per_device(depth, vorticity, legendre_table, pair_slots, diffusion):
    levels, _, band, width = vorticity.shape
    slots, columns = legendre_table.shape[1:]
    blocks = lax.axis_size("lon")
    waves = columns - 1
    cw = min(128, waves)
    half, hops, tiles, pad = blocks // 2, depth // 2, waves // cw, 32
    rows = 2 * tiles * levels + levels
    count = 2 * min(CUTS, tiles)
    dims = (blocks, depth, levels, band, width, slots, waves, cw)
    twid = jnp.asarray(twiddles(blocks, width, waves))
    dma = pltpu.SemaphoreType.DMA
    any_spec, smem = pl.BlockSpec(memory_space=pltpu.HBM), pl.BlockSpec(memory_space=pltpu.SMEM)
    result = pl.pallas_call(
        functools.partial(kernel, dims),
        out_shape=jax.ShapeDtypeStruct((slots, levels, 2, columns), F32),
        in_specs=[smem, smem, any_spec, any_spec, any_spec],
        out_specs=any_spec,
        scratch_shapes=[
            pltpu.VMEM((2 * levels * band, width), F32),
            pltpu.VMEM((tiles + 1, (band + 1) * slots, cw), F32),
            pltpu.VMEM((band * slots, 1), F32),
            pltpu.VMEM(twid.shape, F32),
            pltpu.VMEM((2, *twid.shape), BF16),
            pltpu.VMEM((slots, 3 * pad, waves + cw), BF16),
            pltpu.VMEM((blocks, band, width), F32),
            pltpu.VMEM((blocks, band, width), F32),
            pltpu.VMEM((waves // 2, 4 * pad), F32),
            pltpu.VMEM((waves // 2, 4 * pad), F32),
            pltpu.VMEM((waves // 2 + slots, 4 * pad), F32),
            pltpu.VMEM((slots, rows, cw), F32),
            pltpu.VMEM((depth, rows, cw), F32),
            pltpu.VMEM((2, hops, rows, cw), F32),
            pltpu.VMEM((slots, rows, cw), F32),
            pltpu.VMEM((slots, levels, 2, columns), F32),
            dma((2,)),
            dma((tiles + 1,)),
            dma((slots,)),
            dma((blocks,)),
            dma((blocks,)),
            dma((blocks,)),
            dma((blocks,)),
            dma((depth,)),
            dma((depth,)),
            dma((2, hops, count)),
            dma((2, hops, count)),
            dma((2, hops, count)),
            dma((2, hops, count)),
            dma((depth, count)),
            dma((depth, count)),
        ],
        compiler_params=pltpu.CompilerParams(
            collective_id=0, has_side_effects=True, vmem_limit_bytes=61 * 1024 * 1024
        ),
    )(
        pair_slots,
        diffusion,
        vorticity.reshape(2 * levels * band, width),
        legendre_table.reshape(band * slots, columns),
        twid,
    )
    groups = 8
    return pl.pallas_call(
        functools.partial(hand_over, groups),
        out_shape=jax.ShapeDtypeStruct(result.shape, F32),
        in_specs=[any_spec],
        out_specs=any_spec,
        scratch_shapes=[pltpu.VMEM(result.shape, F32), dma((groups,)), dma((groups,))],
        compiler_params=pltpu.CompilerParams(vmem_limit_bytes=61 * 1024 * 1024),
    )(result)


def solution(mesh):
    placed = (P(None, None, "lat", "lon"), P("lat", "lon", None), P(), P())
    return jax.shard_map(
        functools.partial(per_device, mesh.shape["lat"] // 2),
        mesh=mesh,
        in_specs=placed,
        out_specs=P("lon", None, None, None),
        check_vma=False,
    )
```

```python
import functools
import math

import jax
import jax.numpy as jnp
import numpy as np
from jax import lax
from jax.experimental import pallas as pl
from jax.experimental.pallas import tpu as pltpu
from jax.sharding import PartitionSpec as P

MESH = pl.DeviceIdType.MESH
CUTS = 1
MEET = (0, 2, 4, 6)
F32 = jnp.float32
BF16 = jnp.bfloat16


def real_dft(parts):
    n = len(parts)
    if n == 1:
        return [(parts[0], None)]
    even, odd = real_dft(parts[0::2]), real_dft(parts[1::2])
    out = [None] * (n // 2 + 1)
    for k in range(n // 4 + 1):
        er, ei = even[k]
        orr, oi = odd[k]
        if k == 0:
            out[0] = (er + orr, None)
            out[n // 2] = (er - orr, None)
        elif 4 * k == n:
            out[k] = (er, -orr)
        else:
            c, s = math.cos(2 * math.pi * k / n), math.sin(2 * math.pi * k / n)
            tr, ti = c * orr, -s * orr
            if oi is not None:
                tr, ti = tr + s * oi, ti + c * oi
            ei = 0.0 if ei is None else ei
            out[k] = (er + tr, ei + ti)
            out[n // 2 - k] = (er - tr, ti - ei)
    return out


def class_blocks(k, blocks):
    rows = [(0, k, 0, 0), (0, k, 1, 0), (1, blocks - 1 - k, 0, 0), (1, blocks - 1 - k, 1, 0)]
    if 0 < k < blocks // 2:
        rows += [(0, blocks - k, 0, 1), (0, blocks - k, 1, 1), (1, k - 1, 0, 1), (1, k - 1, 1, 1)]
    return rows


def twiddles(blocks, width, waves):
    full = blocks * width
    per_class = waves // 2 // blocks
    half = blocks // 2
    table = np.zeros((2 * half, 8 * per_class, width))
    position = np.arange(width)
    for k in range(half + 1):
        for at, (second, residue, part, conj) in enumerate(class_blocks(k, blocks)):
            pair = np.arange(per_class) * blocks + residue
            wave = waves - 1 - pair if second else pair
            angle = 2 * np.pi * ((wave[:, None] * position[None, :]) % full) / full
            cos, sin = np.cos(angle) / math.sqrt(full), np.sin(angle) / math.sqrt(full)
            sign = -1.0 if conj else 1.0
            rows = slice(at * per_class, (at + 1) * per_class)
            table[k, rows] = -sin if part else cos
            if 0 < k < half:
                table[half + k, rows] = sign * (cos if part else sin)
    return table.astype(np.float32)


def split(values):
    high = values.astype(BF16)
    return high, (values - high.astype(F32)).astype(BF16)


def dot_t(a, b):
    return lax.dot_general(a, b, (((1,), (1,)), ((), ())), preferred_element_type=F32)


def kernel(
    dims, pair_ref, diff_ref, vort_hbm, table_hbm, twid_hbm, out_hbm,
    vort, table, tail, twid, twid_split, cat, s1, r1, g, s2, r2, part, sib, ring, final, spread,
    load_sem, tab_sem, out_sem, s1_send, s1_recv, s2_send, s2_recv, sib_send, sib_recv,
    rs_send, rs_recv, ag_send, ag_recv, as_send, as_recv,
):
    blocks, depth, levels, band, width, slots, waves, cw = dims
    half, hops = blocks // 2, depth // 2
    tiles = waves // cw
    pad = 32
    per_class = waves // 2 // blocks
    main_rows = 2 * tiles * levels
    cut = min(CUTS, tiles)
    size = main_rows // 2 // cut
    pieces = [(k * size, size, hops - k // cut) for k in range(2 * cut)]
    pieces[-1] = (pieces[-1][0], size + levels, hops - 1)

    meet = [c for c in MEET if c < hops]

    def parent(d):
        return max(c for c in meet if c < d)

    def children(c):
        return sorted((d for d in range(1, hops + 1) if parent(d) == c), reverse=True)

    me = lax.axis_index("lon")
    lat = lax.axis_index("lat")
    z, core = lat // 2, lat % 2
    other = 1 - core

    def at_z(step):
        return lax.rem(z + step + depth, depth)

    def z_device(step):
        return (me, at_z(step) * 2 + core)

    sibling = (me, z * 2 + other)

    load = pltpu.make_async_copy(vort_hbm, vort, load_sem.at[0])
    load.start()
    load_twid = pltpu.make_async_copy(twid_hbm, twid, load_sem.at[1])
    load_twid.start()

    def table_copy(k):
        if k == tiles:
            return pltpu.make_async_copy(table_hbm.at[:, pl.ds(waves, 1)], tail, tab_sem.at[k])
        return pltpu.make_async_copy(
            table_hbm.at[:, pl.ds(k * cw, cw)], table.at[k, pl.ds(0, band * slots)], tab_sem.at[k]
        )

    for k in range(tiles + 1):
        table_copy(k).start()

    barrier = pltpu.get_barrier_semaphore()

    def greet(k, carry):
        peer = lax.rem(me + k, blocks)
        pl.semaphore_signal(barrier, inc=1, device_id=(peer, lat), device_id_type=MESH)
        return carry

    lax.fori_loop(1, blocks, greet, 0)
    near = sorted({sign * (d - parent(d)) for d in range(1, hops + 1) for sign in (1, -1)})
    for target in [z_device(step) for step in near] + [sibling]:
        pl.semaphore_signal(barrier, inc=1, device_id=target, device_id_type=MESH)

    load.wait()
    for level in range(levels):
        north = vort[pl.ds(2 * level * band, band), :]
        south = vort[pl.ds((2 * level + 1) * band, band), :]
        s1[level] = north + south
        s1[levels + level] = north - south

    pl.semaphore_wait(barrier, blocks + len(near))

    def send1(k):
        peer = lax.rem(me + k, blocks)
        return pltpu.make_async_remote_copy(
            src_ref=s1.at[peer], dst_ref=r1.at[me], send_sem=s1_send.at[peer],
            recv_sem=s1_recv.at[me], device_id=(peer, lat), device_id_type=MESH,
        )

    def recv1(k):
        peer = lax.rem(me + k, blocks)
        return pltpu.make_async_remote_copy(
            src_ref=s1.at[peer], dst_ref=r1.at[peer], send_sem=s1_send.at[peer],
            recv_sem=s1_recv.at[peer], device_id=(peer, lat), device_id_type=MESH,
        )

    def loop(low, high, body):
        def step(k, carry):
            body(k)
            return carry

        lax.fori_loop(low, high, step, 0)

    loop(1, blocks, lambda k: send1(k).start())
    r1[me] = s1[me]

    for k in range(tiles + 1):
        table_copy(k).wait()
    table[tiles, pl.ds(0, band * slots), :] = jnp.broadcast_to(tail[...], (band * slots, cw))

    def stack_table(s):
        for k in range(tiles + 1):
            rows = table[k, pl.ds(s, band, stride=slots), :]
            if band < pad:
                rows = jnp.concatenate([rows, jnp.zeros((pad - band, cw), F32)], axis=0)
            high, low = split(rows)
            lanes = pl.ds(k * cw, cw)
            cat[s, pl.ds(0, pad), lanes] = high
            cat[s, pl.ds(pad, pad), lanes] = high
            cat[s, pl.ds(2 * pad, pad), lanes] = low

    load_twid.wait()

    def split_twiddles(k):
        high, low = split(twid[k])
        twid_split[0, k] = high
        twid_split[1, k] = low

    loop(0, 2 * half, split_twiddles)
    loop(0, slots * 3 // 8, stack_table)
    loop(1, blocks, lambda k: recv1(k).wait_recv())

    spectrum = real_dft([r1[a] for a in range(blocks)])
    for k in range(half + 1):
        rows = class_blocks(k, blocks)
        count = len(rows) * per_class
        total = None
        for number, value in ((k, spectrum[k][0]), (half + k, spectrum[k][1])):
            if value is None:
                continue
            if band < pad:
                value = jnp.concatenate([value, jnp.zeros((pad - band, width), F32)], axis=0)
            high, low = split(value)
            w_high = twid_split[0, number, pl.ds(0, count), :]
            w_low = twid_split[1, number, pl.ds(0, count), :]
            term = dot_t(w_high, high) + (dot_t(w_high, low) + dot_t(w_low, high))
            total = term if total is None else total + term
        for at, (second, residue, which, _) in enumerate(rows):
            g[pl.ds(residue * per_class, per_class), pl.ds((2 * second + which) * pad, pad)] = total[
                at * per_class : (at + 1) * per_class
            ]

    unroll = 8

    def gather(i):
        for j in range(unroll):
            pair = pair_ref[i * unroll + j]
            row = (pair & (blocks - 1)) * per_class + (pair >> (blocks.bit_length() - 1))
            s2[pl.ds(i * unroll + j, 1), :] = g[pl.ds(row, 1), :]

    loop(0, waves // 2 // unroll, gather)

    def block_of(index):
        return pl.ds(pl.multiple_of(index * slots, 8), slots)

    def copy2(k, incoming):
        peer = lax.rem(me + k, blocks)
        return pltpu.make_async_remote_copy(
            src_ref=s2.at[block_of(peer)], dst_ref=r2.at[block_of(peer if incoming else me)],
            send_sem=s2_send.at[peer], recv_sem=s2_recv.at[peer if incoming else me],
            device_id=(peer, lat), device_id_type=MESH,
        )

    loop(1, blocks, lambda k: copy2(k, False).start())
    r2[block_of(me), :] = s2[block_of(me), :]
    loop(slots * 3 // 8, slots, stack_table)
    loop(1, blocks, lambda k: copy2(k, True).wait_recv())

    def legendre(s):
        x = r2[pl.ds(s, blocks, stride=slots), :]
        turned = [x] + [pltpu.roll(x, shift=pad * k, axis=1) for k in range(1, 4)]
        high = [t.astype(BF16).astype(F32) for t in turned]
        low = [t - h for t, h in zip(turned, high)]
        lane = lax.broadcasted_iota(jnp.int32, x.shape, 1)
        operand = jnp.concatenate(
            [
                jnp.where(lane < pad, high[-q % 4], jnp.where(lane < 2 * pad, low[(1 - q) % 4], high[(2 - q) % 4]))
                for q in range(4)
            ],
            axis=0,
        ).astype(BF16)[:, : 3 * pad]
        pair = pair_ref[me * slots + s]
        step = 2 * cw
        for n in range(0, waves + cw, step):
            size = min(step, waves + cw - n)
            sums = jnp.dot(operand, cat[s, :, pl.ds(n, size)], preferred_element_type=F32)
            for k in range(size // cw):
                column = n + k * cw + lax.broadcasted_iota(jnp.int32, (levels, cw), 1)
                if n + k * cw == waves:
                    column = jnp.full((levels, cw), waves, jnp.int32)
                second = column >= waves - pair
                odd = (jnp.where(second, column + pair, column) & 1) == 1
                chosen = []
                for r in range(2):
                    pick = [
                        sums[(2 * w + r) * 2 * levels + p * levels :][:levels, k * cw : (k + 1) * cw]
                        for w in range(2)
                        for p in range(2)
                    ]
                    chosen.append(
                        jnp.where(second, jnp.where(odd, pick[3], pick[2]), jnp.where(odd, pick[1], pick[0]))
                    )
                if n + k * cw == waves:
                    side = lax.broadcasted_iota(jnp.int32, (levels, cw), 1) < cw // 2
                    part[s, pl.ds(main_rows, levels), :] = jnp.where(side, chosen[0], chosen[1])
                else:
                    for r in range(2):
                        row = (r * tiles + n // cw + k) * levels
                        part[s, pl.ds(row, levels), :] = chosen[r]

    def sib_copy(owner):
        return pltpu.make_async_remote_copy(
            src_ref=part.at[2 * owner + other], dst_ref=sib.at[owner], send_sem=sib_send.at[owner],
            recv_sem=sib_recv.at[owner], device_id=sibling, device_id_type=MESH,
        )

    def owner_at(way, d):
        return at_z(d if way == 0 else -d)

    def reach(way, p):
        return pieces[p][2] if way == 0 else depth - 1 - pieces[p][2]

    def prepare(d):
        count = 2 if 0 < d < hops else 1

        def one(i):
            sign = 1 - 2 * lax.rem(i, count)
            owner = at_z(sign * d)
            away = i < count
            slot = 2 * owner + jnp.where(away, other, core)
            legendre(slot)

            @pl.when(away)
            def _():
                sib_copy(owner).start()

        loop(0, 2 * count, one)

    def ring_copy(way, d, p):
        low, rows, _ = pieces[p]
        slot = 2 * owner_at(way, d) + core
        hop = d - parent(d)
        return pltpu.make_async_remote_copy(
            src_ref=part.at[slot, pl.ds(low, rows)], dst_ref=ring.at[way, d - 1, pl.ds(low, rows)],
            send_sem=rs_send.at[way, d - 1, p], recv_sem=rs_recv.at[way, d - 1, p],
            device_id=z_device(hop if way == 0 else -hop), device_id_type=MESH,
        )

    def pass_on(d):
        sib_copy(owner_at(0, d)).wait_recv()
        if d < hops:
            sib_copy(owner_at(1, d)).wait_recv()
        for p in range(len(pieces)):
            low, rows, _ = pieces[p]
            for way in range(2):
                if d > reach(way, p):
                    continue
                owner = owner_at(way, d)
                value = part[2 * owner + core, pl.ds(low, rows), :] + sib[owner, pl.ds(low, rows), :]
                for child in children(d) if d in meet else ():
                    if child <= reach(way, p):
                        ring_copy(way, child, p).wait_recv()
                        value = value + ring[way, child - 1, pl.ds(low, rows), :]
                part[2 * owner + core, pl.ds(low, rows), :] = value
                ring_copy(way, d, p).start()

    waiting = []
    for d in range(hops, -1, -1):
        prepare(d)
        alone = [late for late in waiting if late not in meet or not children(late)]
        joined = [late for late in waiting if late not in alone and (d == 0 or late == meet[-1] and late - d >= 3)]
        for late in alone + joined:
            pass_on(late)
            waiting.remove(late)
        if d:
            waiting.append(d)

    mine = 2 * z + core
    sib_copy(z).wait_recv()
    pair = pair_ref[me * slots + mine]
    level_of = lax.broadcasted_iota(jnp.int32, (levels, cw), 0)
    strength = jnp.zeros((levels, cw), F32)
    for level in range(levels):
        strength = jnp.where(level_of == level, diff_ref[level], strength)

    def damping(column):
        degree = jnp.where(column >= waves - pair, column - 1, pair + column).astype(F32)
        ratio = degree * (degree + 1.0) / float((waves - 1) * waves)
        return 1.0 / (1.0 + strength * (ratio * ratio))

    def ag_copy(way, d, p):
        low, rows, _ = pieces[p]
        hop = d - parent(d)
        slot = 2 * owner_at(1 - way, parent(d)) + core
        return pltpu.make_async_remote_copy(
            src_ref=final.at[slot, pl.ds(low, rows)], dst_ref=final.at[slot, pl.ds(low, rows)],
            send_sem=ag_send.at[way, d - 1, p], recv_sem=ag_recv.at[way, d - 1, p],
            device_id=z_device(hop if way == 0 else -hop), device_id_type=MESH,
        )

    def as_copy(owner, p, side):
        low, rows, _ = pieces[p]
        slot = 2 * owner + side
        return pltpu.make_async_remote_copy(
            src_ref=final.at[slot, pl.ds(low, rows)], dst_ref=final.at[slot, pl.ds(low, rows)],
            send_sem=as_send.at[owner, p], recv_sem=as_recv.at[owner, p],
            device_id=sibling, device_id_type=MESH,
        )

    def go_on(way, d, p):
        for child in children(d) if d in meet else ():
            if child <= reach(way, p):
                ag_copy(way, child, p).start()

    def lay_out(slot, p):
        low, rows, _ = pieces[p]
        for row in range(low, min(low + rows, main_rows), levels):
            k = (row // levels) % tiles
            spread[slot, :, row // (tiles * levels), pl.ds(k * cw, cw)] = final[slot, pl.ds(row, levels), :]
        if low + rows > main_rows:
            last = final[slot, pl.ds(main_rows, levels), :]
            spread[slot, :, 0, pl.ds(waves, 1)] = last[:, 0:1]
            spread[slot, :, 1, pl.ds(waves, 1)] = last[:, cw // 2 : cw // 2 + 1]

    def out_copy(slot):
        return pltpu.make_async_copy(spread.at[slot], out_hbm.at[slot], out_sem.at[slot])

    for p in range(len(pieces)):
        low, rows, _ = pieces[p]
        for way in range(2):
            for child in children(0):
                if child <= reach(way, p):
                    ring_copy(way, child, p).wait_recv()
        for row in range(low, low + rows, levels):
            piece = pl.ds(row, levels)
            value = part[mine, piece, :] + sib[z, piece, :]
            for way in range(2):
                for child in (c for c in children(0) if c <= reach(way, p)):
                    value = value + ring[way, child - 1, piece, :]
            if row >= main_rows:
                column = jnp.full((levels, cw), waves, jnp.int32)
            else:
                first = (row // levels) % tiles * cw
                column = first + lax.broadcasted_iota(jnp.int32, (levels, cw), 1)
            final[mine, piece, :] = value * damping(column)
        for way in range(2):
            go_on(way, 0, p)
        as_copy(z, p, core).start()

    def finish(d):
        for way in range(2 if 0 < d < hops else 1):
            owner = owner_at(way, d)
            for p in range(len(pieces)):
                as_copy(owner, p, other).wait_recv()
                lay_out(2 * owner + core, p)
                lay_out(2 * owner + other, p)
            out_copy(2 * owner + core).start()
            out_copy(2 * owner + other).start()

    done = [0]
    order = sorted(range(1, hops + 1), key=lambda d: d - 1.5 * (d in meet and bool(children(d)) or d == hops))
    for d in order:
        for p in range(len(pieces)):
            for way in range(2):
                if d <= reach(way, p):
                    ag_copy(way, d, p).wait_recv()
                    go_on(way, d, p)
                    as_copy(owner_at(1 - way, d), p, core).start()
        finish(done[-1])
        done.append(d)
    finish(done[-1])

    def settle_owner(owner):
        sib_copy(owner).wait_send()
        for p in range(len(pieces)):
            as_copy(owner, p, core).wait_send()

    loop(0, depth, settle_owner)

    def settle_peer(k):
        send1(k).wait_send()
        copy2(k, False).wait_send()

    loop(1, blocks, settle_peer)
    for way in range(2):
        for p in range(len(pieces)):
            for d in range(1, reach(way, p) + 1):
                ring_copy(way, d, p).wait_send()
                ag_copy(way, d, p).wait_send()
    loop(0, slots, lambda slot: out_copy(slot).wait())


def hand_over(groups, source, target, held, in_sem, out_sem):
    size = source.shape[0] // groups
    parts = [pl.ds(k * size, size) for k in range(groups)]
    reads = [pltpu.make_async_copy(source.at[at], held.at[at], in_sem.at[k]) for k, at in enumerate(parts)]
    writes = [pltpu.make_async_copy(held.at[at], target.at[at], out_sem.at[k]) for k, at in enumerate(parts)]
    for read in reads:
        read.start()
    for read, write in zip(reads, writes):
        read.wait()
        write.start()
    for write in writes:
        write.wait()


def per_device(depth, vorticity, legendre_table, pair_slots, diffusion):
    levels, _, band, width = vorticity.shape
    slots, columns = legendre_table.shape[1:]
    blocks = lax.axis_size("lon")
    waves = columns - 1
    cw = min(128, waves)
    half, hops, tiles, pad = blocks // 2, depth // 2, waves // cw, 32
    rows = 2 * tiles * levels + levels
    count = 2 * min(CUTS, tiles)
    dims = (blocks, depth, levels, band, width, slots, waves, cw)
    twid = jnp.asarray(twiddles(blocks, width, waves))
    dma = pltpu.SemaphoreType.DMA
    any_spec, smem = pl.BlockSpec(memory_space=pltpu.HBM), pl.BlockSpec(memory_space=pltpu.SMEM)
    result = pl.pallas_call(
        functools.partial(kernel, dims),
        out_shape=jax.ShapeDtypeStruct((slots, levels, 2, columns), F32),
        in_specs=[smem, smem, any_spec, any_spec, any_spec],
        out_specs=any_spec,
        scratch_shapes=[
            pltpu.VMEM((2 * levels * band, width), F32),
            pltpu.VMEM((tiles + 1, (band + 1) * slots, cw), F32),
            pltpu.VMEM((band * slots, 1), F32),
            pltpu.VMEM(twid.shape, F32),
            pltpu.VMEM((2, *twid.shape), BF16),
            pltpu.VMEM((slots, 3 * pad, waves + cw), BF16),
            pltpu.VMEM((blocks, band, width), F32),
            pltpu.VMEM((blocks, band, width), F32),
            pltpu.VMEM((waves // 2, 4 * pad), F32),
            pltpu.VMEM((waves // 2, 4 * pad), F32),
            pltpu.VMEM((waves // 2 + slots, 4 * pad), F32),
            pltpu.VMEM((slots, rows, cw), F32),
            pltpu.VMEM((depth, rows, cw), F32),
            pltpu.VMEM((2, hops, rows, cw), F32),
            pltpu.VMEM((slots, rows, cw), F32),
            pltpu.VMEM((slots, levels, 2, columns), F32),
            dma((2,)),
            dma((tiles + 1,)),
            dma((slots,)),
            dma((blocks,)),
            dma((blocks,)),
            dma((blocks,)),
            dma((blocks,)),
            dma((depth,)),
            dma((depth,)),
            dma((2, hops, count)),
            dma((2, hops, count)),
            dma((2, hops, count)),
            dma((2, hops, count)),
            dma((depth, count)),
            dma((depth, count)),
        ],
        compiler_params=pltpu.CompilerParams(
            collective_id=0, has_side_effects=True, vmem_limit_bytes=61 * 1024 * 1024
        ),
    )(
        pair_slots,
        diffusion,
        vorticity.reshape(2 * levels * band, width),
        legendre_table.reshape(band * slots, columns),
        twid,
    )
    groups = 8
    return pl.pallas_call(
        functools.partial(hand_over, groups),
        out_shape=jax.ShapeDtypeStruct(result.shape, F32),
        in_specs=[any_spec],
        out_specs=any_spec,
        scratch_shapes=[pltpu.VMEM(result.shape, F32), dma((groups,)), dma((groups,))],
        compiler_params=pltpu.CompilerParams(vmem_limit_bytes=61 * 1024 * 1024),
    )(result)


def solution(mesh):
    placed = (P(None, None, "lat", "lon"), P("lat", "lon", None), P(), P())
    return jax.shard_map(
        functools.partial(per_device, mesh.shape["lat"] // 2),
        mesh=mesh,
        in_specs=placed,
        out_specs=P("lon", None, None, None),
        check_vma=False,
    )
```

```python
import functools
import math

import jax
import jax.numpy as jnp
import numpy as np
from jax import lax
from jax.experimental import pallas as pl
from jax.experimental.pallas import tpu as pltpu
from jax.sharding import PartitionSpec as P

MESH = pl.DeviceIdType.MESH
CUTS = 1
MEET = (0, 2, 4, 6)
F32 = jnp.float32
BF16 = jnp.bfloat16


def real_dft(parts):
    n = len(parts)
    if n == 1:
        return [(parts[0], None)]
    even, odd = real_dft(parts[0::2]), real_dft(parts[1::2])
    out = [None] * (n // 2 + 1)
    for k in range(n // 4 + 1):
        er, ei = even[k]
        orr, oi = odd[k]
        if k == 0:
            out[0] = (er + orr, None)
            out[n // 2] = (er - orr, None)
        elif 4 * k == n:
            out[k] = (er, -orr)
        else:
            c, s = math.cos(2 * math.pi * k / n), math.sin(2 * math.pi * k / n)
            tr, ti = c * orr, -s * orr
            if oi is not None:
                tr, ti = tr + s * oi, ti + c * oi
            ei = 0.0 if ei is None else ei
            out[k] = (er + tr, ei + ti)
            out[n // 2 - k] = (er - tr, ti - ei)
    return out


def class_blocks(k, blocks):
    rows = [(0, k, 0, 0), (0, k, 1, 0), (1, blocks - 1 - k, 0, 0), (1, blocks - 1 - k, 1, 0)]
    if 0 < k < blocks // 2:
        rows += [(0, blocks - k, 0, 1), (0, blocks - k, 1, 1), (1, k - 1, 0, 1), (1, k - 1, 1, 1)]
    return rows


def twiddles(blocks, width, waves):
    full = blocks * width
    per_class = waves // 2 // blocks
    half = blocks // 2
    table = np.zeros((2 * half, 8 * per_class, width))
    position = np.arange(width)
    for k in range(half + 1):
        for at, (second, residue, part, conj) in enumerate(class_blocks(k, blocks)):
            pair = np.arange(per_class) * blocks + residue
            wave = waves - 1 - pair if second else pair
            angle = 2 * np.pi * ((wave[:, None] * position[None, :]) % full) / full
            cos, sin = np.cos(angle) / math.sqrt(full), np.sin(angle) / math.sqrt(full)
            sign = -1.0 if conj else 1.0
            rows = slice(at * per_class, (at + 1) * per_class)
            table[k, rows] = -sin if part else cos
            if 0 < k < half:
                table[half + k, rows] = sign * (cos if part else sin)
    return table.astype(np.float32)


def split(values):
    high = values.astype(BF16)
    return high, (values - high.astype(F32)).astype(BF16)


def dot_t(a, b):
    return lax.dot_general(a, b, (((1,), (1,)), ((), ())), preferred_element_type=F32)


def kernel(
    dims, pair_ref, diff_ref, vort_hbm, table_hbm, twid_hbm, out_hbm,
    vort, table, tail, twid, twid_split, cat, s1, r1, g, s2, r2, part, sib, ring, final, spread,
    load_sem, tab_sem, out_sem, s1_send, s1_recv, s2_send, s2_recv, sib_send, sib_recv,
    rs_send, rs_recv, ag_send, ag_recv, as_send, as_recv,
):
    blocks, depth, levels, band, width, slots, waves, cw = dims
    half, hops = blocks // 2, depth // 2
    tiles = waves // cw
    pad = 32
    per_class = waves // 2 // blocks
    main_rows = 2 * tiles * levels
    cut = min(CUTS, tiles)
    size = main_rows // 2 // cut
    pieces = [(k * size, size, hops - k // cut) for k in range(2 * cut)]
    pieces[-1] = (pieces[-1][0], size + levels, hops - 1)

    meet = [c for c in MEET if c < hops]

    def parent(d):
        return max(c for c in meet if c < d)

    def children(c):
        return sorted((d for d in range(1, hops + 1) if parent(d) == c), reverse=True)

    me = lax.axis_index("lon")
    lat = lax.axis_index("lat")
    z, core = lat // 2, lat % 2
    other = 1 - core

    def at_z(step):
        return lax.rem(z + step + depth, depth)

    def z_device(step):
        return (me, at_z(step) * 2 + core)

    sibling = (me, z * 2 + other)

    load = pltpu.make_async_copy(vort_hbm, vort, load_sem.at[0])
    load.start()
    load_twid = pltpu.make_async_copy(twid_hbm, twid, load_sem.at[1])
    load_twid.start()

    def table_copy(k):
        if k == tiles:
            return pltpu.make_async_copy(table_hbm.at[:, pl.ds(waves, 1)], tail, tab_sem.at[k])
        return pltpu.make_async_copy(
            table_hbm.at[:, pl.ds(k * cw, cw)], table.at[k, pl.ds(0, band * slots)], tab_sem.at[k]
        )

    for k in range(tiles + 1):
        table_copy(k).start()

    barrier = pltpu.get_barrier_semaphore()

    def greet(k, carry):
        peer = lax.rem(me + k, blocks)
        pl.semaphore_signal(barrier, inc=1, device_id=(peer, lat), device_id_type=MESH)
        return carry

    lax.fori_loop(1, blocks, greet, 0)
    near = sorted({sign * (d - parent(d)) for d in range(1, hops + 1) for sign in (1, -1)})
    for target in [z_device(step) for step in near] + [sibling]:
        pl.semaphore_signal(barrier, inc=1, device_id=target, device_id_type=MESH)

    load.wait()
    for level in range(levels):
        north = vort[pl.ds(2 * level * band, band), :]
        south = vort[pl.ds((2 * level + 1) * band, band), :]
        s1[level] = north + south
        s1[levels + level] = north - south

    pl.semaphore_wait(barrier, blocks + len(near))

    def send1(k):
        peer = lax.rem(me + k, blocks)
        return pltpu.make_async_remote_copy(
            src_ref=s1.at[peer], dst_ref=r1.at[me], send_sem=s1_send.at[peer],
            recv_sem=s1_recv.at[me], device_id=(peer, lat), device_id_type=MESH,
        )

    def recv1(k):
        peer = lax.rem(me + k, blocks)
        return pltpu.make_async_remote_copy(
            src_ref=s1.at[peer], dst_ref=r1.at[peer], send_sem=s1_send.at[peer],
            recv_sem=s1_recv.at[peer], device_id=(peer, lat), device_id_type=MESH,
        )

    def loop(low, high, body):
        def step(k, carry):
            body(k)
            return carry

        lax.fori_loop(low, high, step, 0)

    loop(1, blocks, lambda k: send1(k).start())
    r1[me] = s1[me]

    for k in range(tiles + 1):
        table_copy(k).wait()
    table[tiles, pl.ds(0, band * slots), :] = jnp.broadcast_to(tail[...], (band * slots, cw))

    def stack_table(s):
        for k in range(tiles + 1):
            rows = table[k, pl.ds(s, band, stride=slots), :]
            if band < pad:
                rows = jnp.concatenate([rows, jnp.zeros((pad - band, cw), F32)], axis=0)
            high, low = split(rows)
            lanes = pl.ds(k * cw, cw)
            cat[s, pl.ds(0, pad), lanes] = high
            cat[s, pl.ds(pad, pad), lanes] = high
            cat[s, pl.ds(2 * pad, pad), lanes] = low

    load_twid.wait()

    def split_twiddles(k):
        high, low = split(twid[k])
        twid_split[0, k] = high
        twid_split[1, k] = low

    loop(0, 2 * half, split_twiddles)
    def stack_tables(i):
        for k in range(4):
            stack_table(4 * i + k)

    early = slots * 3 // 32
    loop(0, early, stack_tables)
    loop(1, blocks, lambda k: recv1(k).wait_recv())

    spectrum = real_dft([r1[a] for a in range(blocks)])
    for k in range(half + 1):
        rows = class_blocks(k, blocks)
        count = len(rows) * per_class
        total = None
        for number, value in ((k, spectrum[k][0]), (half + k, spectrum[k][1])):
            if value is None:
                continue
            if band < pad:
                value = jnp.concatenate([value, jnp.zeros((pad - band, width), F32)], axis=0)
            high, low = split(value)
            w_high = twid_split[0, number, pl.ds(0, count), :]
            w_low = twid_split[1, number, pl.ds(0, count), :]
            term = dot_t(w_high, high) + (dot_t(w_high, low) + dot_t(w_low, high))
            total = term if total is None else total + term
        for at, (second, residue, which, _) in enumerate(rows):
            g[pl.ds(residue * per_class, per_class), pl.ds((2 * second + which) * pad, pad)] = total[
                at * per_class : (at + 1) * per_class
            ]

    unroll = 8

    def gather(i):
        for j in range(unroll):
            pair = pair_ref[i * unroll + j]
            row = (pair & (blocks - 1)) * per_class + (pair >> (blocks.bit_length() - 1))
            s2[pl.ds(i * unroll + j, 1), :] = g[pl.ds(row, 1), :]

    loop(0, waves // 2 // unroll, gather)

    def block_of(index):
        return pl.ds(pl.multiple_of(index * slots, 8), slots)

    def copy2(k, incoming):
        peer = lax.rem(me + k, blocks)
        return pltpu.make_async_remote_copy(
            src_ref=s2.at[block_of(peer)], dst_ref=r2.at[block_of(peer if incoming else me)],
            send_sem=s2_send.at[peer], recv_sem=s2_recv.at[peer if incoming else me],
            device_id=(peer, lat), device_id_type=MESH,
        )

    loop(1, blocks, lambda k: copy2(k, False).start())
    r2[block_of(me), :] = s2[block_of(me), :]
    loop(early, slots // 4, stack_tables)
    loop(1, blocks, lambda k: copy2(k, True).wait_recv())

    def operand_of(s):
        x = r2[pl.ds(s, blocks, stride=slots), :]
        turned = [x] + [pltpu.roll(x, shift=pad * k, axis=1) for k in range(1, 4)]
        high = [t.astype(BF16).astype(F32) for t in turned]
        low = [t - h for t, h in zip(turned, high)]
        lane = lax.broadcasted_iota(jnp.int32, x.shape, 1)
        return jnp.concatenate(
            [
                jnp.where(lane < pad, high[-q % 4], jnp.where(lane < 2 * pad, low[(1 - q) % 4], high[(2 - q) % 4]))
                for q in range(4)
            ],
            axis=0,
        ).astype(BF16)[:, : 3 * pad]

    def choose(s, pair, n, size, sums):
        for k in range(size // cw):
            column = n + k * cw + lax.broadcasted_iota(jnp.int32, (levels, cw), 1)
            if n + k * cw == waves:
                column = jnp.full((levels, cw), waves, jnp.int32)
            second = column >= waves - pair
            odd = (jnp.where(second, column + pair, column) & 1) == 1
            chosen = []
            for r in range(2):
                pick = [
                    sums[(2 * w + r) * 2 * levels + p * levels :][:levels, k * cw : (k + 1) * cw]
                    for w in range(2)
                    for p in range(2)
                ]
                chosen.append(
                    jnp.where(second, jnp.where(odd, pick[3], pick[2]), jnp.where(odd, pick[1], pick[0]))
                )
            if n + k * cw == waves:
                side = lax.broadcasted_iota(jnp.int32, (levels, cw), 1) < cw // 2
                part[s, pl.ds(main_rows, levels), :] = jnp.where(side, chosen[0], chosen[1])
            else:
                for r in range(2):
                    row = (r * tiles + n // cw + k) * levels
                    part[s, pl.ds(row, levels), :] = chosen[r]

    def legendre(some):
        operands = [operand_of(s) for s in some]
        pairs = [pair_ref[me * slots + s] for s in some]
        step = 2 * cw
        for n in range(0, waves + cw, step):
            size = min(step, waves + cw - n)
            sums = [
                jnp.dot(operand, cat[s, :, pl.ds(n, size)], preferred_element_type=F32)
                for s, operand in zip(some, operands)
            ]
            for s, pair, value in zip(some, pairs, sums):
                choose(s, pair, n, size, value)

    def sib_copy(owner):
        return pltpu.make_async_remote_copy(
            src_ref=part.at[2 * owner + other], dst_ref=sib.at[owner], send_sem=sib_send.at[owner],
            recv_sem=sib_recv.at[owner], device_id=sibling, device_id_type=MESH,
        )

    def owner_at(way, d):
        return at_z(d if way == 0 else -d)

    def reach(way, p):
        return pieces[p][2] if way == 0 else depth - 1 - pieces[p][2]

    def prepare(d):
        def one(i):
            owner = at_z(d - 2 * d * i)
            legendre([2 * owner + other, 2 * owner + core])
            sib_copy(owner).start()

        if 0 < d < hops:
            loop(0, 2, one)
        else:
            one(0)

    def ring_copy(way, d, p):
        low, rows, _ = pieces[p]
        slot = 2 * owner_at(way, d) + core
        hop = d - parent(d)
        return pltpu.make_async_remote_copy(
            src_ref=part.at[slot, pl.ds(low, rows)], dst_ref=ring.at[way, d - 1, pl.ds(low, rows)],
            send_sem=rs_send.at[way, d - 1, p], recv_sem=rs_recv.at[way, d - 1, p],
            device_id=z_device(hop if way == 0 else -hop), device_id_type=MESH,
        )

    def pass_on(d):
        sib_copy(owner_at(0, d)).wait_recv()
        if d < hops:
            sib_copy(owner_at(1, d)).wait_recv()
        for p in range(len(pieces)):
            low, rows, _ = pieces[p]
            for way in range(2):
                if d > reach(way, p):
                    continue
                owner = owner_at(way, d)
                value = part[2 * owner + core, pl.ds(low, rows), :] + sib[owner, pl.ds(low, rows), :]
                for child in children(d) if d in meet else ():
                    if child <= reach(way, p):
                        ring_copy(way, child, p).wait_recv()
                        value = value + ring[way, child - 1, pl.ds(low, rows), :]
                part[2 * owner + core, pl.ds(low, rows), :] = value
                ring_copy(way, d, p).start()

    waiting = []
    for d in range(hops, -1, -1):
        prepare(d)
        alone = [late for late in waiting if late not in meet or not children(late)]
        joined = [late for late in waiting if late not in alone and (d == 0 or late == meet[-1] and late - d >= 3)]
        for late in alone + joined:
            pass_on(late)
            waiting.remove(late)
        if d:
            waiting.append(d)

    mine = 2 * z + core
    sib_copy(z).wait_recv()
    pair = pair_ref[me * slots + mine]
    level_of = lax.broadcasted_iota(jnp.int32, (levels, cw), 0)
    strength = jnp.zeros((levels, cw), F32)
    for level in range(levels):
        strength = jnp.where(level_of == level, diff_ref[level], strength)

    def damping(column):
        degree = jnp.where(column >= waves - pair, column - 1, pair + column).astype(F32)
        ratio = degree * (degree + 1.0) / float((waves - 1) * waves)
        return 1.0 / (1.0 + strength * (ratio * ratio))

    def ag_copy(way, d, p):
        low, rows, _ = pieces[p]
        hop = d - parent(d)
        slot = 2 * owner_at(1 - way, parent(d)) + core
        return pltpu.make_async_remote_copy(
            src_ref=final.at[slot, pl.ds(low, rows)], dst_ref=final.at[slot, pl.ds(low, rows)],
            send_sem=ag_send.at[way, d - 1, p], recv_sem=ag_recv.at[way, d - 1, p],
            device_id=z_device(hop if way == 0 else -hop), device_id_type=MESH,
        )

    def as_copy(owner, p, side):
        low, rows, _ = pieces[p]
        slot = 2 * owner + side
        return pltpu.make_async_remote_copy(
            src_ref=final.at[slot, pl.ds(low, rows)], dst_ref=final.at[slot, pl.ds(low, rows)],
            send_sem=as_send.at[owner, p], recv_sem=as_recv.at[owner, p],
            device_id=sibling, device_id_type=MESH,
        )

    def go_on(way, d, p):
        for child in children(d) if d in meet else ():
            if child <= reach(way, p):
                ag_copy(way, child, p).start()

    def lay_out(slot, p):
        low, rows, _ = pieces[p]
        for row in range(low, min(low + rows, main_rows), levels):
            k = (row // levels) % tiles
            spread[slot, :, row // (tiles * levels), pl.ds(k * cw, cw)] = final[slot, pl.ds(row, levels), :]
        if low + rows > main_rows:
            last = final[slot, pl.ds(main_rows, levels), :]
            spread[slot, :, 0, pl.ds(waves, 1)] = last[:, 0:1]
            spread[slot, :, 1, pl.ds(waves, 1)] = last[:, cw // 2 : cw // 2 + 1]

    def out_copy(slot):
        return pltpu.make_async_copy(spread.at[slot], out_hbm.at[slot], out_sem.at[slot])

    for p in range(len(pieces)):
        low, rows, _ = pieces[p]
        for way in range(2):
            for child in children(0):
                if child <= reach(way, p):
                    ring_copy(way, child, p).wait_recv()
        for row in range(low, low + rows, levels):
            piece = pl.ds(row, levels)
            value = part[mine, piece, :] + sib[z, piece, :]
            for way in range(2):
                for child in (c for c in children(0) if c <= reach(way, p)):
                    value = value + ring[way, child - 1, piece, :]
            if row >= main_rows:
                column = jnp.full((levels, cw), waves, jnp.int32)
            else:
                first = (row // levels) % tiles * cw
                column = first + lax.broadcasted_iota(jnp.int32, (levels, cw), 1)
            final[mine, piece, :] = value * damping(column)
        for way in range(2):
            go_on(way, 0, p)
        as_copy(z, p, core).start()

    def finish(d):
        for way in range(2 if 0 < d < hops else 1):
            owner = owner_at(way, d)
            for p in range(len(pieces)):
                as_copy(owner, p, other).wait_recv()
                lay_out(2 * owner + core, p)
                lay_out(2 * owner + other, p)
            out_copy(2 * owner + core).start()
            out_copy(2 * owner + other).start()

    done = [0]
    order = sorted(range(1, hops + 1), key=lambda d: d - 1.5 * (d in meet and bool(children(d)) or d == hops))
    for d in order:
        for p in range(len(pieces)):
            for way in range(2):
                if d <= reach(way, p):
                    ag_copy(way, d, p).wait_recv()
                    go_on(way, d, p)
                    as_copy(owner_at(1 - way, d), p, core).start()
        finish(done[-1])
        done.append(d)
    finish(done[-1])

    def settle_owner(owner):
        sib_copy(owner).wait_send()
        for p in range(len(pieces)):
            as_copy(owner, p, core).wait_send()

    loop(0, depth, settle_owner)

    def settle_peer(k):
        send1(k).wait_send()
        copy2(k, False).wait_send()

    loop(1, blocks, settle_peer)
    for way in range(2):
        for p in range(len(pieces)):
            for d in range(1, reach(way, p) + 1):
                ring_copy(way, d, p).wait_send()
                ag_copy(way, d, p).wait_send()
    loop(0, slots, lambda slot: out_copy(slot).wait())


def hand_over(groups, source, target, held, in_sem, out_sem):
    size = source.shape[0] // groups
    parts = [pl.ds(k * size, size) for k in range(groups)]
    reads = [pltpu.make_async_copy(source.at[at], held.at[at], in_sem.at[k]) for k, at in enumerate(parts)]
    writes = [pltpu.make_async_copy(held.at[at], target.at[at], out_sem.at[k]) for k, at in enumerate(parts)]
    for read in reads:
        read.start()
    for read, write in zip(reads, writes):
        read.wait()
        write.start()
    for write in writes:
        write.wait()


def per_device(depth, vorticity, legendre_table, pair_slots, diffusion):
    levels, _, band, width = vorticity.shape
    slots, columns = legendre_table.shape[1:]
    blocks = lax.axis_size("lon")
    waves = columns - 1
    cw = min(128, waves)
    half, hops, tiles, pad = blocks // 2, depth // 2, waves // cw, 32
    rows = 2 * tiles * levels + levels
    count = 2 * min(CUTS, tiles)
    dims = (blocks, depth, levels, band, width, slots, waves, cw)
    twid = jnp.asarray(twiddles(blocks, width, waves))
    dma = pltpu.SemaphoreType.DMA
    any_spec, smem = pl.BlockSpec(memory_space=pltpu.HBM), pl.BlockSpec(memory_space=pltpu.SMEM)
    result = pl.pallas_call(
        functools.partial(kernel, dims),
        out_shape=jax.ShapeDtypeStruct((slots, levels, 2, columns), F32),
        in_specs=[smem, smem, any_spec, any_spec, any_spec],
        out_specs=any_spec,
        scratch_shapes=[
            pltpu.VMEM((2 * levels * band, width), F32),
            pltpu.VMEM((tiles + 1, (band + 1) * slots, cw), F32),
            pltpu.VMEM((band * slots, 1), F32),
            pltpu.VMEM(twid.shape, F32),
            pltpu.VMEM((2, *twid.shape), BF16),
            pltpu.VMEM((slots, 3 * pad, waves + cw), BF16),
            pltpu.VMEM((blocks, band, width), F32),
            pltpu.VMEM((blocks, band, width), F32),
            pltpu.VMEM((waves // 2, 4 * pad), F32),
            pltpu.VMEM((waves // 2, 4 * pad), F32),
            pltpu.VMEM((waves // 2 + slots, 4 * pad), F32),
            pltpu.VMEM((slots, rows, cw), F32),
            pltpu.VMEM((depth, rows, cw), F32),
            pltpu.VMEM((2, hops, rows, cw), F32),
            pltpu.VMEM((slots, rows, cw), F32),
            pltpu.VMEM((slots, levels, 2, columns), F32),
            dma((2,)),
            dma((tiles + 1,)),
            dma((slots,)),
            dma((blocks,)),
            dma((blocks,)),
            dma((blocks,)),
            dma((blocks,)),
            dma((depth,)),
            dma((depth,)),
            dma((2, hops, count)),
            dma((2, hops, count)),
            dma((2, hops, count)),
            dma((2, hops, count)),
            dma((depth, count)),
            dma((depth, count)),
        ],
        compiler_params=pltpu.CompilerParams(
            collective_id=0, has_side_effects=True, vmem_limit_bytes=61 * 1024 * 1024
        ),
    )(
        pair_slots,
        diffusion,
        vorticity.reshape(2 * levels * band, width),
        legendre_table.reshape(band * slots, columns),
        twid,
    )
    groups = 8
    return pl.pallas_call(
        functools.partial(hand_over, groups),
        out_shape=jax.ShapeDtypeStruct(result.shape, F32),
        in_specs=[any_spec],
        out_specs=any_spec,
        scratch_shapes=[pltpu.VMEM(result.shape, F32), dma((groups,)), dma((groups,))],
        compiler_params=pltpu.CompilerParams(vmem_limit_bytes=61 * 1024 * 1024),
    )(result)


def solution(mesh):
    placed = (P(None, None, "lat", "lon"), P("lat", "lon", None), P(), P())
    return jax.shard_map(
        functools.partial(per_device, mesh.shape["lat"] // 2),
        mesh=mesh,
        in_specs=placed,
        out_specs=P("lon", None, None, None),
        check_vma=False,
    )
```

```python
import functools
import math

import jax
import jax.numpy as jnp
import numpy as np
from jax import lax
from jax.experimental import pallas as pl
from jax.experimental.pallas import tpu as pltpu
from jax.sharding import PartitionSpec as P

MESH = pl.DeviceIdType.MESH
CUTS = 1
MEET = (0, 2, 4, 6)
F32 = jnp.float32
BF16 = jnp.bfloat16


def real_dft(parts):
    n = len(parts)
    if n == 1:
        return [(parts[0], None)]
    even, odd = real_dft(parts[0::2]), real_dft(parts[1::2])
    out = [None] * (n // 2 + 1)
    for k in range(n // 4 + 1):
        er, ei = even[k]
        orr, oi = odd[k]
        if k == 0:
            out[0] = (er + orr, None)
            out[n // 2] = (er - orr, None)
        elif 4 * k == n:
            out[k] = (er, -orr)
        else:
            c, s = math.cos(2 * math.pi * k / n), math.sin(2 * math.pi * k / n)
            tr, ti = c * orr, -s * orr
            if oi is not None:
                tr, ti = tr + s * oi, ti + c * oi
            ei = 0.0 if ei is None else ei
            out[k] = (er + tr, ei + ti)
            out[n // 2 - k] = (er - tr, ti - ei)
    return out


def class_blocks(k, blocks):
    rows = [(0, k, 0, 0), (0, k, 1, 0), (1, blocks - 1 - k, 0, 0), (1, blocks - 1 - k, 1, 0)]
    if 0 < k < blocks // 2:
        rows += [(0, blocks - k, 0, 1), (0, blocks - k, 1, 1), (1, k - 1, 0, 1), (1, k - 1, 1, 1)]
    return rows


def twiddles(blocks, width, waves):
    full = blocks * width
    per_class = waves // 2 // blocks
    half = blocks // 2
    table = np.zeros((2 * half, 8 * per_class, width))
    position = np.arange(width)
    for k in range(half + 1):
        for at, (second, residue, part, conj) in enumerate(class_blocks(k, blocks)):
            pair = np.arange(per_class) * blocks + residue
            wave = waves - 1 - pair if second else pair
            angle = 2 * np.pi * ((wave[:, None] * position[None, :]) % full) / full
            cos, sin = np.cos(angle) / math.sqrt(full), np.sin(angle) / math.sqrt(full)
            sign = -1.0 if conj else 1.0
            rows = slice(at * per_class, (at + 1) * per_class)
            table[k, rows] = -sin if part else cos
            if 0 < k < half:
                table[half + k, rows] = sign * (cos if part else sin)
    return table.astype(np.float32)


def split(values):
    high = values.astype(BF16)
    return high, (values - high.astype(F32)).astype(BF16)


def dot_t(a, b):
    return lax.dot_general(a, b, (((1,), (1,)), ((), ())), preferred_element_type=F32)


def kernel(
    dims, pair_ref, diff_ref, vort_hbm, table_hbm, twid_hbm, out_hbm,
    vort, table, tail, twid, twid_split, cat, s1, r1, g, s2, r2, part, sib, ring, final, spread,
    load_sem, tab_sem, out_sem, s1_send, s1_recv, s2_send, s2_recv, sib_send, sib_recv,
    rs_send, rs_recv, ag_send, ag_recv, as_send, as_recv,
):
    blocks, depth, levels, band, width, slots, waves, cw = dims
    half, hops = blocks // 2, depth // 2
    tiles = waves // cw
    pad = 32
    per_class = waves // 2 // blocks
    main_rows = 2 * tiles * levels
    cut = min(CUTS, tiles)
    size = main_rows // 2 // cut
    pieces = [(k * size, size, hops - k // cut) for k in range(2 * cut)]
    pieces[-1] = (pieces[-1][0], size + levels, hops - 1)

    meet = [c for c in MEET if c < hops]

    def parent(d):
        return max(c for c in meet if c < d)

    def children(c):
        return sorted((d for d in range(1, hops + 1) if parent(d) == c), reverse=True)

    me = lax.axis_index("lon")
    lat = lax.axis_index("lat")
    z, core = lat // 2, lat % 2
    other = 1 - core

    def at_z(step):
        return lax.rem(z + step + depth, depth)

    def z_device(step):
        return (me, at_z(step) * 2 + core)

    sibling = (me, z * 2 + other)

    load = pltpu.make_async_copy(vort_hbm, vort, load_sem.at[0])
    load.start()
    load_twid = pltpu.make_async_copy(twid_hbm, twid, load_sem.at[1])
    load_twid.start()

    def table_copy(k):
        if k == tiles:
            return pltpu.make_async_copy(table_hbm.at[:, pl.ds(waves, 1)], tail, tab_sem.at[k])
        return pltpu.make_async_copy(
            table_hbm.at[:, pl.ds(k * cw, cw)], table.at[k, pl.ds(0, band * slots)], tab_sem.at[k]
        )

    for k in range(tiles + 1):
        table_copy(k).start()

    barrier = pltpu.get_barrier_semaphore()

    def greet(k, carry):
        peer = lax.rem(me + k, blocks)
        pl.semaphore_signal(barrier, inc=1, device_id=(peer, lat), device_id_type=MESH)
        return carry

    lax.fori_loop(1, blocks, greet, 0)
    near = sorted({sign * (d - parent(d)) for d in range(1, hops + 1) for sign in (1, -1)})
    for target in [z_device(step) for step in near] + [sibling]:
        pl.semaphore_signal(barrier, inc=1, device_id=target, device_id_type=MESH)

    load.wait()
    for level in range(levels):
        north = vort[pl.ds(2 * level * band, band), :]
        south = vort[pl.ds((2 * level + 1) * band, band), :]
        s1[level] = north + south
        s1[levels + level] = north - south

    pl.semaphore_wait(barrier, blocks + len(near))

    def send1(k):
        peer = lax.rem(me + k, blocks)
        return pltpu.make_async_remote_copy(
            src_ref=s1.at[peer], dst_ref=r1.at[me], send_sem=s1_send.at[peer],
            recv_sem=s1_recv.at[me], device_id=(peer, lat), device_id_type=MESH,
        )

    def recv1(k):
        peer = lax.rem(me + k, blocks)
        return pltpu.make_async_remote_copy(
            src_ref=s1.at[peer], dst_ref=r1.at[peer], send_sem=s1_send.at[peer],
            recv_sem=s1_recv.at[peer], device_id=(peer, lat), device_id_type=MESH,
        )

    def loop(low, high, body):
        def step(k, carry):
            body(k)
            return carry

        lax.fori_loop(low, high, step, 0)

    loop(1, blocks, lambda k: send1(k).start())
    r1[me] = s1[me]

    for k in range(tiles + 1):
        table_copy(k).wait()
    table[tiles, pl.ds(0, band * slots), :] = jnp.broadcast_to(tail[...], (band * slots, cw))

    def stack_table(s):
        for k in range(tiles + 1):
            rows = table[k, pl.ds(s, band, stride=slots), :]
            if band < pad:
                rows = jnp.concatenate([rows, jnp.zeros((pad - band, cw), F32)], axis=0)
            high, low = split(rows)
            lanes = pl.ds(k * cw, cw)
            cat[s, pl.ds(0, pad), lanes] = high
            cat[s, pl.ds(pad, pad), lanes] = high
            cat[s, pl.ds(2 * pad, pad), lanes] = low

    load_twid.wait()

    def split_twiddles(k):
        high, low = split(twid[k])
        twid_split[0, k] = high
        twid_split[1, k] = low

    loop(0, 2 * half, split_twiddles)
    def stack_tables(i):
        for k in range(4):
            stack_table(4 * i + k)

    early = slots * 3 // 32
    loop(0, early, stack_tables)
    loop(1, blocks, lambda k: recv1(k).wait_recv())

    spectrum = real_dft([r1[a] for a in range(blocks)])
    for k in range(half + 1):
        rows = class_blocks(k, blocks)
        count = len(rows) * per_class
        total = None
        for number, value in ((k, spectrum[k][0]), (half + k, spectrum[k][1])):
            if value is None:
                continue
            if band < pad:
                value = jnp.concatenate([value, jnp.zeros((pad - band, width), F32)], axis=0)
            high, low = split(value)
            w_high = twid_split[0, number, pl.ds(0, count), :]
            w_low = twid_split[1, number, pl.ds(0, count), :]
            both = dot_t(w_high, jnp.concatenate([high, low], axis=0))
            cross = dot_t(w_low, high)
            total = (both, cross) if total is None else (total[0] + both, total[1] + cross)
        total = total[0][:, :pad] + (total[0][:, pad:] + total[1])
        for at, (second, residue, which, _) in enumerate(rows):
            g[pl.ds(residue * per_class, per_class), pl.ds((2 * second + which) * pad, pad)] = total[
                at * per_class : (at + 1) * per_class
            ]

    unroll = 8

    def gather(i):
        for j in range(unroll):
            pair = pair_ref[i * unroll + j]
            row = (pair & (blocks - 1)) * per_class + (pair >> (blocks.bit_length() - 1))
            s2[pl.ds(i * unroll + j, 1), :] = g[pl.ds(row, 1), :]

    loop(0, waves // 2 // unroll, gather)

    def block_of(index):
        return pl.ds(pl.multiple_of(index * slots, 8), slots)

    def copy2(k, incoming):
        peer = lax.rem(me + k, blocks)
        return pltpu.make_async_remote_copy(
            src_ref=s2.at[block_of(peer)], dst_ref=r2.at[block_of(peer if incoming else me)],
            send_sem=s2_send.at[peer], recv_sem=s2_recv.at[peer if incoming else me],
            device_id=(peer, lat), device_id_type=MESH,
        )

    loop(1, blocks, lambda k: copy2(k, False).start())
    r2[block_of(me), :] = s2[block_of(me), :]
    loop(early, slots // 4, stack_tables)
    loop(1, blocks, lambda k: copy2(k, True).wait_recv())

    def operand_of(s):
        x = r2[pl.ds(s, blocks, stride=slots), :]
        turned = [x] + [pltpu.roll(x, shift=pad * k, axis=1) for k in range(1, 4)]
        high = [t.astype(BF16).astype(F32) for t in turned]
        low = [t - h for t, h in zip(turned, high)]
        lane = lax.broadcasted_iota(jnp.int32, x.shape, 1)
        return jnp.concatenate(
            [
                jnp.where(lane < pad, high[-q % 4], jnp.where(lane < 2 * pad, low[(1 - q) % 4], high[(2 - q) % 4]))
                for q in range(4)
            ],
            axis=0,
        ).astype(BF16)[:, : 3 * pad]

    def choose(s, pair, n, size, sums):
        for k in range(size // cw):
            column = n + k * cw + lax.broadcasted_iota(jnp.int32, (levels, cw), 1)
            if n + k * cw == waves:
                column = jnp.full((levels, cw), waves, jnp.int32)
            second = column >= waves - pair
            odd = (jnp.where(second, column + pair, column) & 1) == 1
            chosen = []
            for r in range(2):
                pick = [
                    sums[(2 * w + r) * 2 * levels + p * levels :][:levels, k * cw : (k + 1) * cw]
                    for w in range(2)
                    for p in range(2)
                ]
                chosen.append(
                    jnp.where(second, jnp.where(odd, pick[3], pick[2]), jnp.where(odd, pick[1], pick[0]))
                )
            if n + k * cw == waves:
                side = lax.broadcasted_iota(jnp.int32, (levels, cw), 1) < cw // 2
                part[s, pl.ds(main_rows, levels), :] = jnp.where(side, chosen[0], chosen[1])
            else:
                for r in range(2):
                    row = (r * tiles + n // cw + k) * levels
                    part[s, pl.ds(row, levels), :] = chosen[r]

    def legendre(some):
        operands = [operand_of(s) for s in some]
        pairs = [pair_ref[me * slots + s] for s in some]
        step = 2 * cw
        for n in range(0, waves + cw, step):
            size = min(step, waves + cw - n)
            sums = [
                jnp.dot(operand, cat[s, :, pl.ds(n, size)], preferred_element_type=F32)
                for s, operand in zip(some, operands)
            ]
            for s, pair, value in zip(some, pairs, sums):
                choose(s, pair, n, size, value)

    def sib_copy(owner):
        return pltpu.make_async_remote_copy(
            src_ref=part.at[2 * owner + other], dst_ref=sib.at[owner], send_sem=sib_send.at[owner],
            recv_sem=sib_recv.at[owner], device_id=sibling, device_id_type=MESH,
        )

    def owner_at(way, d):
        return at_z(d if way == 0 else -d)

    def reach(way, p):
        return pieces[p][2] if way == 0 else depth - 1 - pieces[p][2]

    def prepare(d):
        def one(i):
            owner = at_z(d - 2 * d * i)
            legendre([2 * owner + other, 2 * owner + core])
            sib_copy(owner).start()

        if 0 < d < hops:
            loop(0, 2, one)
        else:
            one(0)

    def ring_copy(way, d, p):
        low, rows, _ = pieces[p]
        slot = 2 * owner_at(way, d) + core
        hop = d - parent(d)
        return pltpu.make_async_remote_copy(
            src_ref=part.at[slot, pl.ds(low, rows)], dst_ref=ring.at[way, d - 1, pl.ds(low, rows)],
            send_sem=rs_send.at[way, d - 1, p], recv_sem=rs_recv.at[way, d - 1, p],
            device_id=z_device(hop if way == 0 else -hop), device_id_type=MESH,
        )

    def pass_on(d):
        sib_copy(owner_at(0, d)).wait_recv()
        if d < hops:
            sib_copy(owner_at(1, d)).wait_recv()
        for p in range(len(pieces)):
            low, rows, _ = pieces[p]
            for way in range(2):
                if d > reach(way, p):
                    continue
                owner = owner_at(way, d)
                value = part[2 * owner + core, pl.ds(low, rows), :] + sib[owner, pl.ds(low, rows), :]
                for child in children(d) if d in meet else ():
                    if child <= reach(way, p):
                        ring_copy(way, child, p).wait_recv()
                        value = value + ring[way, child - 1, pl.ds(low, rows), :]
                part[2 * owner + core, pl.ds(low, rows), :] = value
                ring_copy(way, d, p).start()

    waiting = []
    for d in range(hops, -1, -1):
        prepare(d)
        alone = [late for late in waiting if late not in meet or not children(late)]
        joined = [late for late in waiting if late not in alone and (d == 0 or late == meet[-1] and late - d >= 3)]
        for late in alone + joined:
            pass_on(late)
            waiting.remove(late)
        if d:
            waiting.append(d)

    mine = 2 * z + core
    sib_copy(z).wait_recv()
    pair = pair_ref[me * slots + mine]
    level_of = lax.broadcasted_iota(jnp.int32, (levels, cw), 0)
    strength = jnp.zeros((levels, cw), F32)
    for level in range(levels):
        strength = jnp.where(level_of == level, diff_ref[level], strength)

    def damping(column):
        degree = jnp.where(column >= waves - pair, column - 1, pair + column).astype(F32)
        ratio = degree * (degree + 1.0) / float((waves - 1) * waves)
        return 1.0 / (1.0 + strength * (ratio * ratio))

    def ag_copy(way, d, p):
        low, rows, _ = pieces[p]
        hop = d - parent(d)
        slot = 2 * owner_at(1 - way, parent(d)) + core
        return pltpu.make_async_remote_copy(
            src_ref=final.at[slot, pl.ds(low, rows)], dst_ref=final.at[slot, pl.ds(low, rows)],
            send_sem=ag_send.at[way, d - 1, p], recv_sem=ag_recv.at[way, d - 1, p],
            device_id=z_device(hop if way == 0 else -hop), device_id_type=MESH,
        )

    def as_copy(owner, p, side):
        low, rows, _ = pieces[p]
        slot = 2 * owner + side
        return pltpu.make_async_remote_copy(
            src_ref=final.at[slot, pl.ds(low, rows)], dst_ref=final.at[slot, pl.ds(low, rows)],
            send_sem=as_send.at[owner, p], recv_sem=as_recv.at[owner, p],
            device_id=sibling, device_id_type=MESH,
        )

    def go_on(way, d, p):
        for child in children(d) if d in meet else ():
            if child <= reach(way, p):
                ag_copy(way, child, p).start()

    def lay_out(slot, p):
        low, rows, _ = pieces[p]
        for row in range(low, min(low + rows, main_rows), levels):
            k = (row // levels) % tiles
            spread[slot, :, row // (tiles * levels), pl.ds(k * cw, cw)] = final[slot, pl.ds(row, levels), :]
        if low + rows > main_rows:
            last = final[slot, pl.ds(main_rows, levels), :]
            spread[slot, :, 0, pl.ds(waves, 1)] = last[:, 0:1]
            spread[slot, :, 1, pl.ds(waves, 1)] = last[:, cw // 2 : cw // 2 + 1]

    def out_copy(slot):
        return pltpu.make_async_copy(spread.at[slot], out_hbm.at[slot], out_sem.at[slot])

    for p in range(len(pieces)):
        low, rows, _ = pieces[p]
        for way in range(2):
            for child in children(0):
                if child <= reach(way, p):
                    ring_copy(way, child, p).wait_recv()
        for row in range(low, low + rows, levels):
            piece = pl.ds(row, levels)
            value = part[mine, piece, :] + sib[z, piece, :]
            for way in range(2):
                for child in (c for c in children(0) if c <= reach(way, p)):
                    value = value + ring[way, child - 1, piece, :]
            if row >= main_rows:
                column = jnp.full((levels, cw), waves, jnp.int32)
            else:
                first = (row // levels) % tiles * cw
                column = first + lax.broadcasted_iota(jnp.int32, (levels, cw), 1)
            final[mine, piece, :] = value * damping(column)
        for way in range(2):
            go_on(way, 0, p)
        as_copy(z, p, core).start()

    def finish(d):
        for way in range(2 if 0 < d < hops else 1):
            owner = owner_at(way, d)
            for p in range(len(pieces)):
                as_copy(owner, p, other).wait_recv()
                lay_out(2 * owner + core, p)
                lay_out(2 * owner + other, p)
            out_copy(2 * owner + core).start()
            out_copy(2 * owner + other).start()

    done = [0]
    order = sorted(range(1, hops + 1), key=lambda d: d - 1.5 * (d in meet and bool(children(d)) or d == hops))
    for d in order:
        for p in range(len(pieces)):
            for way in range(2):
                if d <= reach(way, p):
                    ag_copy(way, d, p).wait_recv()
                    go_on(way, d, p)
                    as_copy(owner_at(1 - way, d), p, core).start()
        finish(done[-1])
        done.append(d)
    finish(done[-1])

    def settle_owner(owner):
        sib_copy(owner).wait_send()
        for p in range(len(pieces)):
            as_copy(owner, p, core).wait_send()

    loop(0, depth, settle_owner)

    def settle_peer(k):
        send1(k).wait_send()
        copy2(k, False).wait_send()

    loop(1, blocks, settle_peer)
    for way in range(2):
        for p in range(len(pieces)):
            for d in range(1, reach(way, p) + 1):
                ring_copy(way, d, p).wait_send()
                ag_copy(way, d, p).wait_send()
    loop(0, slots, lambda slot: out_copy(slot).wait())


def hand_over(groups, source, target, held, in_sem, out_sem):
    size = source.shape[0] // groups
    parts = [pl.ds(k * size, size) for k in range(groups)]
    reads = [pltpu.make_async_copy(source.at[at], held.at[at], in_sem.at[k]) for k, at in enumerate(parts)]
    writes = [pltpu.make_async_copy(held.at[at], target.at[at], out_sem.at[k]) for k, at in enumerate(parts)]
    for read in reads:
        read.start()
    for read, write in zip(reads, writes):
        read.wait()
        write.start()
    for write in writes:
        write.wait()


def per_device(depth, vorticity, legendre_table, pair_slots, diffusion):
    levels, _, band, width = vorticity.shape
    slots, columns = legendre_table.shape[1:]
    blocks = lax.axis_size("lon")
    waves = columns - 1
    cw = min(128, waves)
    half, hops, tiles, pad = blocks // 2, depth // 2, waves // cw, 32
    rows = 2 * tiles * levels + levels
    count = 2 * min(CUTS, tiles)
    dims = (blocks, depth, levels, band, width, slots, waves, cw)
    twid = jnp.asarray(twiddles(blocks, width, waves))
    dma = pltpu.SemaphoreType.DMA
    any_spec, smem = pl.BlockSpec(memory_space=pltpu.HBM), pl.BlockSpec(memory_space=pltpu.SMEM)
    result = pl.pallas_call(
        functools.partial(kernel, dims),
        out_shape=jax.ShapeDtypeStruct((slots, levels, 2, columns), F32),
        in_specs=[smem, smem, any_spec, any_spec, any_spec],
        out_specs=any_spec,
        scratch_shapes=[
            pltpu.VMEM((2 * levels * band, width), F32),
            pltpu.VMEM((tiles + 1, (band + 1) * slots, cw), F32),
            pltpu.VMEM((band * slots, 1), F32),
            pltpu.VMEM(twid.shape, F32),
            pltpu.VMEM((2, *twid.shape), BF16),
            pltpu.VMEM((slots, 3 * pad, waves + cw), BF16),
            pltpu.VMEM((blocks, band, width), F32),
            pltpu.VMEM((blocks, band, width), F32),
            pltpu.VMEM((waves // 2, 4 * pad), F32),
            pltpu.VMEM((waves // 2, 4 * pad), F32),
            pltpu.VMEM((waves // 2 + slots, 4 * pad), F32),
            pltpu.VMEM((slots, rows, cw), F32),
            pltpu.VMEM((depth, rows, cw), F32),
            pltpu.VMEM((2, hops, rows, cw), F32),
            pltpu.VMEM((slots, rows, cw), F32),
            pltpu.VMEM((slots, levels, 2, columns), F32),
            dma((2,)),
            dma((tiles + 1,)),
            dma((slots,)),
            dma((blocks,)),
            dma((blocks,)),
            dma((blocks,)),
            dma((blocks,)),
            dma((depth,)),
            dma((depth,)),
            dma((2, hops, count)),
            dma((2, hops, count)),
            dma((2, hops, count)),
            dma((2, hops, count)),
            dma((depth, count)),
            dma((depth, count)),
        ],
        compiler_params=pltpu.CompilerParams(
            collective_id=0, has_side_effects=True, vmem_limit_bytes=61 * 1024 * 1024
        ),
    )(
        pair_slots,
        diffusion,
        vorticity.reshape(2 * levels * band, width),
        legendre_table.reshape(band * slots, columns),
        twid,
    )
    groups = 8
    return pl.pallas_call(
        functools.partial(hand_over, groups),
        out_shape=jax.ShapeDtypeStruct(result.shape, F32),
        in_specs=[any_spec],
        out_specs=any_spec,
        scratch_shapes=[pltpu.VMEM(result.shape, F32), dma((groups,)), dma((groups,))],
        compiler_params=pltpu.CompilerParams(vmem_limit_bytes=61 * 1024 * 1024),
    )(result)


def solution(mesh):
    placed = (P(None, None, "lat", "lon"), P("lat", "lon", None), P(), P())
    return jax.shard_map(
        functools.partial(per_device, mesh.shape["lat"] // 2),
        mesh=mesh,
        in_specs=placed,
        out_specs=P("lon", None, None, None),
        check_vma=False,
    )
```
